512 devices in a mesh: seq: 32 (over z_hi, x, core), dp: 16 (over y, z_lo).
Axes of the slice: x: 4, y: 4, z: 16 (z_hi: 4, z_lo: 4; z = z_hi * 4 + z_lo), core: 2. Of those that a mesh axis runs over, the one named last changes fastest.
Arguments:
- queries: bfloat16 [2048, 32, 1024], P('seq', 'dp'), may hold values from -12 to 12
- key_vectors: bfloat16 [2048, 32, 1024], P('seq', 'dp'), may hold values from -12 to 12
- value_vectors: bfloat16 [2048, 32, 1024], P('seq', 'dp'), may hold values from -6 to 6
- features: bfloat16 [2048, 32, 1024], P('seq', 'dp'), may hold values from -6 to 6
- cotangent: bfloat16 [2048, 32, 1024], P('seq', 'dp'), may hold values from -6 to 6
- frames: int32 [32], P('dp'), may hold values from 512 to 2048, as said below
- conv_kernel: float32 [31, 1024], replicated, may hold values from -1 to 1
- conv_bias: float32 [1024], replicated, may hold values from -3 to 3
Outputs:
- block_out: bfloat16 [2048, 32, 1024], P('seq', 'dp')
- grad_features: bfloat16 [2048, 32, 1024], P('seq', 'dp')
- grad_queries: bfloat16 [2048, 32, 1024], P('seq', 'dp')
- grad_keys: bfloat16 [2048, 32, 1024], P('seq', 'dp')
- grad_values: bfloat16 [2048, 32, 1024], P('seq', 'dp')
- grad_kernel: float32 [31, 1024], replicated
- grad_bias: float32 [1024], replicated
The draws below stay inside these ranges and needn't reach their ends.
Inputs may be any that keep to these rules, and one draw needn't show every extreme that they name: Every utterance has at least 512 valid frames, and utterance 0 has all 2048.
All inputs are finite; a program needn't handle non-finite values.
Results may differ from the reference program's by a relative error of at most 0.0065.
Values may be sent and summed in bfloat16 or wider, within the bound.
No kernel may reach another device: no remote copies, remote signals or barrier semaphores. Data moves between devices by JAX's collectives and lax.ppermute only.
A program may use at most 64 MiB of HBM per device.

```python
import math
import jax
import jax.numpy as jnp
from jax import lax

D = 1024
HEADS = 16
TAPS = 31
L = 2048
UTT = 32


def drawn_pair(key):
    full_shape = (L, UTT, D)
    query_seed = jax.random.fold_in(key, 101)
    key_seed = jax.random.fold_in(key, 102)
    scale_seed = jax.random.fold_in(key, 103)
    query_base = jax.random.normal(query_seed, full_shape, jnp.float32)
    key_base = jax.random.normal(key_seed, full_shape, jnp.float32)
    log_low = math.log(0.7)
    log_high = math.log(1.4)
    query_scale = jnp.exp(jax.random.uniform(jax.random.fold_in(scale_seed, 1), (L, UTT, 1), jnp.float32, log_low, log_high))
    key_scale = jnp.exp(jax.random.uniform(jax.random.fold_in(scale_seed, 2), (L, UTT, 1), jnp.float32, log_low, log_high))
    query_part = jnp.clip(1.5 * query_scale * query_base, -12.0, 12.0)
    key_part = jnp.clip(1.5 * key_scale * key_base, -12.0, 12.0)
    return (query_part, key_part)


def draw_queries(key, part):
    return drawn_pair(key)[0].astype(jnp.bfloat16)


def draw_key_vectors(key, part):
    return drawn_pair(key)[1].astype(jnp.bfloat16)


def draw_frames(key, part):
    counts = jax.random.randint(key, (UTT,), L // 4, L + 1)
    return counts.at[0].set(L).astype(jnp.int32)


def block_scale(stream_key, extent, shards, low, largest):
    loudness, own = 1.0, jax.random.fold_in(stream_key, 6)
    for dim, shards_of in shards:
        heights = jnp.exp(jax.random.uniform(jax.random.fold_in(own, dim), (shards_of,), jnp.float32, low / len(shards), largest / len(shards)))
        loudness = loudness * jnp.repeat(heights, extent[dim] // shards_of).reshape([-1 if axis == dim else 1 for axis in range(len(extent))])
    return loudness


def scatter_about(key, shape, width, reach, shards=(), dtype=jnp.bfloat16):
    level = block_scale(key, shape, shards, -0.22, 0.18) if shards else 1.0
    values = jax.random.normal(key, shape, jnp.float32) * width * level
    return jnp.minimum(jnp.maximum(values, -reach), reach).astype(dtype)


def setup_inputs(seed: int = 0) -> dict:
    key_of = jax.random.split(jax.random.key(seed), 9)
    return {
        "queries": draw_queries(jax.random.fold_in(key_of[8], 71), 0),
        "key_vectors": draw_key_vectors(jax.random.fold_in(key_of[8], 71), 0),
        "value_vectors": scatter_about(key_of[2], (L, UTT, D), 1.0, 6.0, ((0, 32), (1, 16))),
        "features": scatter_about(key_of[3], (L, UTT, D), 1.0, 6.0, ((0, 32), (1, 16))),
        "cotangent": scatter_about(key_of[4], (L, UTT, D), 1.0, 6.0, ((0, 32), (1, 16))),
        "frames": draw_frames(jax.random.fold_in(key_of[8], 71), 0),
        "conv_kernel": scatter_about(key_of[6], (TAPS, D), TAPS ** -0.5, 1.0, (), jnp.float32),
        "conv_bias": scatter_about(key_of[7], (D,), 0.5, 3.0, (), jnp.float32),
    }


def round_trip(field):
    return lax.optimization_barrier(field.astype(jnp.bfloat16)).astype(jnp.float32)

def attention_probs(query_rows, key_rows, key_count):
    score_scale = 1.0 / math.sqrt(query_rows.shape[1])
    scores = jnp.dot(query_rows.astype(jnp.float32), key_rows.astype(jnp.float32).T) * score_scale
    allowed = jnp.arange(key_rows.shape[0]) < key_count
    scores = jnp.where(allowed[None, :], scores, -jnp.inf)
    row_max = lax.optimization_barrier(jnp.max(scores, axis=1, keepdims=True))
    exp_scores = jnp.exp(scores - row_max)
    return exp_scores / lax.optimization_barrier(jnp.sum(exp_scores, axis=1, keepdims=True))

def forward_item(packed):
    query_rows, key_rows, value_rows, key_count = packed
    probs_bf = round_trip(attention_probs(query_rows, key_rows, key_count))
    return jnp.dot(probs_bf, value_rows.astype(jnp.float32)).astype(jnp.bfloat16)

def backward_item(packed):
    query_rows, key_rows, value_rows, grad_out, key_count = packed
    head_dim = query_rows.shape[1]
    probs = attention_probs(query_rows, key_rows, key_count)
    probs_bf = round_trip(probs)
    grad_rows = grad_out.astype(jnp.float32)
    grad_probs = jnp.dot(grad_rows, value_rows.astype(jnp.float32).T)
    grad_value = jnp.dot(probs_bf.T, grad_rows)
    row_delta = lax.optimization_barrier(jnp.sum(probs * grad_probs, axis=1, keepdims=True))
    grad_scores = round_trip(probs * (grad_probs - row_delta) * (1.0 / math.sqrt(head_dim)))
    grad_query = jnp.dot(grad_scores, key_rows.astype(jnp.float32))
    grad_key = jnp.dot(grad_scores.T, query_rows.astype(jnp.float32))
    return (grad_query.astype(jnp.bfloat16), grad_key.astype(jnp.bfloat16), grad_value.astype(jnp.bfloat16))

def reference(queries, key_vectors, value_vectors, features, cotangent, frames, conv_kernel, conv_bias):
    seq_len, utt_count, model_width = queries.shape
    head_dim = model_width // HEADS
    rim = TAPS // 2

    def split_items(field):
        return jnp.moveaxis(field.reshape(seq_len, utt_count * HEADS, head_dim), 1, 0)

    def join_items(field):
        return jnp.moveaxis(field, 0, 1).reshape(seq_len, utt_count, model_width)
    item_frames = jnp.repeat(frames, HEADS)
    context = join_items(lax.map(forward_item, (split_items(queries), split_items(key_vectors), split_items(value_vectors), item_frames)))
    hidden = features.astype(jnp.float32) + round_trip(context)
    valid_rows = (jnp.arange(seq_len)[:, None] < frames[None, :])[:, :, None]
    masked = round_trip(jnp.where(valid_rows, hidden, 0.0))
    padded = jnp.pad(masked, ((rim, rim), (0, 0), (0, 0)))
    kernel = conv_kernel.astype(jnp.float32)
    conv_out = conv_bias.astype(jnp.float32)[None, None, :] + jnp.zeros_like(hidden)
    for tap_index in range(TAPS):
        conv_out = conv_out + kernel[tap_index] * padded[tap_index:tap_index + seq_len]
    gate_value = jax.nn.sigmoid(conv_out)
    block_out = (hidden + conv_out * gate_value).astype(jnp.bfloat16)
    grad_conv = cotangent.astype(jnp.float32) * gate_value * (1.0 + conv_out * (1.0 - gate_value))
    grad_padded = jnp.pad(round_trip(grad_conv), ((rim, rim), (0, 0), (0, 0)))
    grad_masked = jnp.zeros_like(hidden)
    for tap_index in range(TAPS):
        offset = TAPS - 1 - tap_index
        grad_masked = grad_masked + kernel[tap_index] * grad_padded[offset:offset + seq_len]
    grad_kernel = jnp.stack([lax.optimization_barrier(jnp.sum(grad_conv * padded[tap_index:tap_index + seq_len], axis=(0, 1))) for tap_index in range(TAPS)])
    grad_bias = lax.optimization_barrier(jnp.sum(grad_conv, axis=(0, 1)))
    grad_features = (cotangent.astype(jnp.float32) + jnp.where(valid_rows, grad_masked, 0.0)).astype(jnp.bfloat16)
    grad_query, grad_key, grad_value = lax.map(backward_item, (split_items(queries), split_items(key_vectors), split_items(value_vectors), split_items(grad_features), item_frames))
    return (block_out, grad_features, join_items(grad_query), join_items(grad_key), join_items(grad_value), grad_kernel, grad_bias)
```

```python
import math

import jax
import jax.numpy as jnp
from jax import lax
from jax.experimental import pallas as pl
from jax.experimental.pallas import tpu as pltpu
from jax.sharding import PartitionSpec as P

HEADS = 16
TAPS = 31
HD = 64
LANES = 128
PAD = 16
QB = 512
KC = 512
F32 = jnp.float32
BF16 = jnp.bfloat16
NEG = -1e30
LOG2E = math.log2(math.e)

VMEM = pl.BlockSpec(memory_space=pltpu.VMEM)
SMEM = pl.BlockSpec(memory_space=pltpu.SMEM)


def params(mib):
    return pltpu.CompilerParams(vmem_limit_bytes=mib * 1024 * 1024)


def lane_pair(low, high):
    return jnp.concatenate([low, high], axis=-1)


def swap_halves(x):
    return pltpu.roll(x, HD, x.ndim - 1)


def lane_ids(shape):
    return lax.broadcasted_iota(jnp.int32, shape, len(shape) - 1)


def pack_pair(a_ref, b_ref, out_ref, u):
    rows = a_ref.shape[0]
    a = a_ref[:, u, :]
    b = b_ref[:, u, :]
    for h in range(HEADS):
        part = slice(h * HD, (h + 1) * HD)
        out_ref[u * HEADS + h, 0:rows, :] = lane_pair(a[:, part], b[:, part])


def pack_qkv_kernel(q_ref, k_ref, v_ref, out_ref):
    rows, utts, _ = q_ref.shape
    for u in range(utts):
        pack_pair(q_ref, k_ref, out_ref, u)
        v = v_ref[:, u, :]
        for h in range(HEADS):
            part = slice(h * HD, (h + 1) * HD)
            out_ref[u * HEADS + h, rows:, :] = lane_pair(
                v[: rows // 2, part], v[rows // 2 :, part]
            )


def pack_fc_kernel(f_ref, c_ref, out_ref):
    for u in range(f_ref.shape[1]):
        pack_pair(f_ref, c_ref, out_ref, u)


def unpack_pair(in_ref, a_ref, b_ref):
    rows, utts, _ = a_ref.shape
    firsts, seconds = [], []
    for u in range(utts):
        blocks = [in_ref[u * HEADS + h, 0:rows, :] for h in range(HEADS)]
        firsts.append(jnp.concatenate([x[:, :HD] for x in blocks], axis=1))
        seconds.append(jnp.concatenate([x[:, HD:] for x in blocks], axis=1))
    a_ref[...] = jnp.stack(firsts, axis=1)
    b_ref[...] = jnp.stack(seconds, axis=1)


def unpack_pair_kernel(in_ref, a_ref, b_ref):
    unpack_pair(in_ref, a_ref, b_ref)


def unpack_qkv_kernel(in_ref, q_ref, k_ref, v_ref):
    unpack_pair(in_ref, q_ref, k_ref)
    rows, utts, _ = v_ref.shape
    values = []
    for u in range(utts):
        blocks = [in_ref[u * HEADS + h, rows:, :] for h in range(HEADS)]
        top = jnp.concatenate([x[:, :HD] for x in blocks], axis=1)
        bottom = jnp.concatenate([x[:, HD:] for x in blocks], axis=1)
        values.append(jnp.concatenate([top, bottom], axis=0))
    v_ref[...] = jnp.stack(values, axis=1)


def value_rows(qkv_ref, rows):
    half = qkv_ref[:, rows:, :]
    full = jnp.concatenate([half, half], axis=1)
    lane = lane_ids(full.shape)
    return full, lane


def spread_values(qkv_ref, rows):
    half = qkv_ref[:, rows:, :].astype(F32)
    sources = half.shape[0]
    swapped = pltpu.roll(half.reshape(-1, LANES), HD, 1).reshape(half.shape)
    return jnp.concatenate([half, swapped], axis=1).reshape(sources * rows, LANES)


def forward_kernel(frames_ref, qkv_ref, e_ref, ctx_ref, kaug, vt, scores):
    rows = qkv_ref.shape[1] * 2 // 3
    sources = qkv_ref.shape[0]
    length = sources * rows
    block = pl.program_id(0)
    per_block = QB // rows

    @pl.when(block == 0)
    def _():
        qk = qkv_ref[:, :rows, :].reshape(length, LANES).astype(F32)
        lane = lane_ids(qk.shape)
        position = lax.broadcasted_iota(jnp.int32, qk.shape, 0)
        bias = jnp.where(position < frames_ref[0], 0.0, NEG)
        tail = jnp.where(lane == HD, bias, 0.0)
        kaug[...] = jnp.where(lane < HD, swap_halves(qk), tail).astype(BF16)
        values = spread_values(qkv_ref, rows)
        values = jnp.where(lane < HD, values, jnp.where(lane == HD, 1.0, 0.0))
        vt[...] = values.T.astype(BF16)

    q = qkv_ref[pl.ds(block * per_block, per_block), :rows, :].reshape(QB, LANES).astype(F32)
    lane = lane_ids(q.shape)
    q = jnp.where(lane < HD, q * 0.125, jnp.where(lane == HD, 1.0, 0.0)).astype(BF16)
    top = None
    for c in range(length // KC):
        part = slice(c * KC, (c + 1) * KC)
        s = lax.dot_general(kaug[part, :], q, (((1,), (1,)), ((), ())), preferred_element_type=F32)
        scores[part, :] = s
        high = jnp.max(s, axis=0, keepdims=True)
        top = high if top is None else jnp.maximum(top, high)
    total = None
    for c in range(length // KC):
        part = slice(c * KC, (c + 1) * KC)
        e = jnp.exp2((scores[part, :] - top) * LOG2E).astype(BF16)
        e_ref[0, part, :] = e
        term = jnp.dot(vt[:, part], e, preferred_element_type=F32)
        total = term if total is None else total + term
    total = total.T
    divisor = total[:, HD : HD + 1]
    ctx_ref[...] = jnp.where(lane < HD, total / divisor, 1.0 / divisor)


def conv_kernel_body(
    frames_ref, fc_ref, ctx_ref, taps_ref, bogf_ref, sums_ref, gaug_ref, field, grad, hid, cot, bo
):
    sources, rows, _ = fc_ref.shape
    length = sources * rows
    half = length // 2
    mid = sources // 2
    step = 64
    steps = half // step
    lane = lane_ids((half, LANES))
    valid = frames_ref[0]
    fc_low = fc_ref[:mid].reshape(half, LANES).astype(F32)
    fc_high = fc_ref[mid:].reshape(half, LANES).astype(F32)
    features = jnp.where(lane < HD, fc_low, swap_halves(fc_high))
    cot[...] = jnp.where(lane < HD, swap_halves(fc_low), fc_high)
    ctx = jnp.where(lane < HD, ctx_ref[:half, :], swap_halves(ctx_ref[half:, :]))
    hidden = features + ctx.astype(BF16).astype(F32)
    hid[...] = hidden
    position = lax.broadcasted_iota(jnp.int32, (half, LANES), 0) + jnp.where(lane < HD, 0, half)
    masked = jnp.where(position < valid, hidden, 0.0).astype(BF16).astype(F32)
    small = lane_ids((PAD, LANES))
    field[PAD : PAD + half, :] = masked
    field[:PAD, :] = jnp.where(small < HD, 0.0, swap_halves(masked[half - PAD :, :]))
    field[PAD + half :, :] = jnp.where(small < HD, swap_halves(masked[:PAD, :]), 0.0)
    sums_ref[...] = jnp.zeros_like(sums_ref)
    bias = taps_ref[TAPS : TAPS + 1, :]

    def forward_step(i, carry):
        base = pl.multiple_of(i * step, step)
        out = jnp.broadcast_to(bias, (step, LANES))
        for k in range(TAPS):
            out = out + taps_ref[k : k + 1, :] * field[pl.ds(base + (k + 1), step), :]
        gate = 1.0 / (1.0 + jnp.exp(-out))
        bo[pl.ds(base, step), :] = hid[pl.ds(base, step), :] + out * gate
        g = cot[pl.ds(base, step), :] * gate * (1.0 + out * (1.0 - gate))
        grad[pl.ds(base + PAD, step), :] = g.astype(BF16).astype(F32)
        for k in range(TAPS):
            term = g * field[pl.ds(base + (k + 1), step), :]
            part = slice(8 * k, 8 * k + 8)
            sums_ref[part, :] += jnp.sum(term.reshape(step // 8, 8, LANES), axis=0)
        part = slice(8 * TAPS, 8 * TAPS + 8)
        sums_ref[part, :] += jnp.sum(g.reshape(step // 8, 8, LANES), axis=0)
        return carry

    lax.fori_loop(0, steps, forward_step, 0)
    grad[:PAD, :] = jnp.where(small < HD, 0.0, swap_halves(grad[half : half + PAD, :]))
    grad[PAD + half :, :] = jnp.where(small < HD, swap_halves(grad[PAD : 2 * PAD, :]), 0.0)
    lane_step = lane_ids((step, LANES))
    rows_step = lax.broadcasted_iota(jnp.int32, (step, LANES), 0)
    place = rows_step + jnp.where(lane_step < HD, 0, half)
    per_step = step // rows

    def augmented(gf, context):
        inverse = context[:, HD : HD + 1]
        gn = (gf * (inverse * 0.125)).astype(BF16).astype(F32)
        delta = jnp.sum(jnp.where(lane_step < HD, gn * context, 0.0), axis=1, keepdims=True)
        upper = delta.astype(BF16).astype(F32)
        tail = jnp.where(lane_step == HD, -upper, jnp.where(lane_step == HD + 1, upper - delta, 0.0))
        return jnp.where(lane_step < HD, gn, tail).astype(BF16)

    def backward_step(i, carry):
        base = pl.multiple_of(i * step, step)
        out = None
        for k in range(TAPS):
            term = taps_ref[k : k + 1, :] * grad[pl.ds(base + (TAPS - k), step), :]
            out = term if out is None else out + term
        out = jnp.where(place + base < valid, out, 0.0)
        gf = (cot[pl.ds(base, step), :] + out).astype(BF16).astype(F32)
        swapped = swap_halves(gf)
        block = bo[pl.ds(base, step), :]
        low = jnp.where(lane_step < HD, block, swapped).astype(BF16)
        high = jnp.where(lane_step < HD, swap_halves(block), gf).astype(BF16)
        at = i * per_step
        bogf_ref[pl.ds(at, per_step)] = low.reshape(per_step, rows, LANES)
        bogf_ref[pl.ds(mid + at, per_step)] = high.reshape(per_step, rows, LANES)
        gaug_ref[pl.ds(base, step), :] = augmented(gf, ctx_ref[pl.ds(base, step), :])
        other = pl.multiple_of(base + half, step)
        gaug_ref[pl.ds(other, step), :] = augmented(swapped, ctx_ref[pl.ds(other, step), :])
        return carry

    lax.fori_loop(0, steps, backward_step, 0)


def backward_kernel(qkv_ref, gaug_ref, e_ref, out_ref, vaug, kt, gq, acc_k, acc_v):
    rows = qkv_ref.shape[1] * 2 // 3
    sources = qkv_ref.shape[0]
    length = sources * rows
    block = pl.program_id(0)
    per_block = QB // rows

    @pl.when(block == 0)
    def _():
        qk = qkv_ref[:, :rows, :].reshape(length, LANES).astype(F32)
        lane = lane_ids(qk.shape)
        kt[...] = jnp.where(lane < HD, swap_halves(qk), 0.0).T.astype(BF16)
        values = spread_values(qkv_ref, rows)
        vaug[...] = jnp.where(lane < HD, values, jnp.where(lane < HD + 2, 1.0, 0.0)).astype(BF16)
        acc_k[...] = jnp.zeros_like(acc_k)
        acc_v[...] = jnp.zeros_like(acc_v)

    q = qkv_ref[pl.ds(block * per_block, per_block), :rows, :].reshape(QB, LANES)
    g = gaug_ref[...]
    total = None
    for c in range(length // KC):
        part = slice(c * KC, (c + 1) * KC)
        e = e_ref[0, part, :]
        dp = lax.dot_general(vaug[part, :], g, (((1,), (1,)), ((), ())), preferred_element_type=F32)
        ds = (e.astype(F32) * dp).astype(BF16)
        acc_v[part, :] += jnp.dot(e, g, preferred_element_type=F32)
        acc_k[part, :] += jnp.dot(ds, q, preferred_element_type=F32)
        term = jnp.dot(kt[:, part], ds, preferred_element_type=F32)
        total = term if total is None else total + term
    gq[pl.ds(pl.multiple_of(block * QB, QB), QB), :] = total.T

    @pl.when(block == length // QB - 1)
    def _():
        lane = lane_ids((length, LANES))
        qk = jnp.where(lane < HD, gq[...], swap_halves(acc_k[...]))
        out_ref[:, :rows, :] = qk.astype(BF16).reshape(sources, rows, LANES)
        gv = acc_v[...] * 8.0
        low = gv.reshape(sources, rows, LANES)[:, : rows // 2, :]
        high = swap_halves(gv).reshape(sources, rows, LANES)[:, rows // 2 :, :]
        pick = lane_ids(low.shape) < HD
        out_ref[:, rows:, :] = jnp.where(pick, low, high).astype(BF16)


def shape_of(*dims, dtype=BF16):
    return jax.ShapeDtypeStruct(dims, dtype)


def pack_qkv(q, k, v):
    rows = q.shape[0]
    items = q.shape[1] * HEADS
    return pl.pallas_call(
        pack_qkv_kernel,
        out_shape=shape_of(items, rows * 3 // 2, LANES),
        in_specs=[VMEM] * 3,
        out_specs=VMEM,
        compiler_params=params(24),
        name="pack_qkv",
    )(q, k, v)


def pack_fc(f, c):
    rows = f.shape[0]
    items = f.shape[1] * HEADS
    return pl.pallas_call(
        pack_fc_kernel,
        out_shape=shape_of(items, rows, LANES),
        in_specs=[VMEM] * 2,
        out_specs=VMEM,
        compiler_params=params(24),
        name="pack_fc",
    )(f, c)


def unpack(kernel, field, rows, utts, count):
    return pl.pallas_call(
        kernel,
        out_shape=[shape_of(rows, utts, HEADS * HD)] * count,
        in_specs=[VMEM],
        out_specs=[VMEM] * count,
        compiler_params=params(24),
        name="unpack%d" % count,
    )(field)


def forward(frames, qkv):
    sources, tall, _ = qkv.shape
    length = sources * (tall * 2 // 3)
    blocks = length // QB
    return pl.pallas_call(
        forward_kernel,
        grid=(blocks,),
        out_shape=[shape_of(blocks, length, QB), shape_of(length, LANES, dtype=F32)],
        in_specs=[SMEM, VMEM],
        out_specs=[
            pl.BlockSpec((1, length, QB), lambda i: (i, 0, 0)),
            pl.BlockSpec((QB, LANES), lambda i: (i, 0)),
        ],
        scratch_shapes=[
            pltpu.VMEM((length, LANES), BF16),
            pltpu.VMEM((LANES, length), BF16),
            pltpu.VMEM((length, QB), F32),
        ],
        compiler_params=params(32),
        cost_estimate=pl.CostEstimate(
            flops=40_000_000_000 // 4, bytes_accessed=10_000_000, transcendentals=length * length
        ),
        name="attention_forward",
    )(frames, qkv)


def conv(frames, fc, ctx, taps):
    sources, rows, _ = fc.shape
    length = sources * rows
    half = length // 2
    return pl.pallas_call(
        conv_kernel_body,
        out_shape=[
            shape_of(sources, rows, LANES),
            shape_of(8 * (TAPS + 1), LANES, dtype=F32),
            shape_of(length, LANES),
        ],
        in_specs=[SMEM, VMEM, VMEM, VMEM],
        out_specs=[VMEM] * 3,
        scratch_shapes=[
            pltpu.VMEM((half + 2 * PAD, LANES), F32),
            pltpu.VMEM((half + 2 * PAD, LANES), F32),
            pltpu.VMEM((half, LANES), F32),
            pltpu.VMEM((half, LANES), F32),
            pltpu.VMEM((half, LANES), F32),
        ],
        compiler_params=params(32),
        name="conv",
    )(frames, fc, ctx, taps)


def backward(qkv, gaug, e):
    sources, tall, _ = qkv.shape
    length = sources * (tall * 2 // 3)
    blocks = length // QB
    return pl.pallas_call(
        backward_kernel,
        grid=(blocks,),
        out_shape=shape_of(sources, tall, LANES),
        in_specs=[
            VMEM,
            pl.BlockSpec((QB, LANES), lambda i: (i, 0)),
            pl.BlockSpec((1, length, QB), lambda i: (i, 0, 0)),
        ],
        out_specs=VMEM,
        scratch_shapes=[
            pltpu.VMEM((length, LANES), BF16),
            pltpu.VMEM((LANES, length), BF16),
            pltpu.VMEM((length, LANES), F32),
            pltpu.VMEM((length, LANES), F32),
            pltpu.VMEM((length, LANES), F32),
        ],
        compiler_params=params(32),
        cost_estimate=pl.CostEstimate(
            flops=20_000_000_000, bytes_accessed=10_000_000, transcendentals=0
        ),
        name="attention_backward",
    )(qkv, gaug, e)


def exchange(field):
    return lax.all_to_all(field, "seq", split_axis=0, concat_axis=0, tiled=True)


def swap(field, axis, bit):
    count = lax.axis_size(axis)
    return lax.ppermute(field, axis, [(i, i ^ bit) for i in range(count)])


def joined(field, axis, bit):
    other = swap(field, axis, bit)
    upper = (lax.axis_index(axis) & bit) != 0
    first = jnp.where(upper, other, field)
    second = jnp.where(upper, field, other)
    return jnp.concatenate([first, second], axis=0)


def reduce_params(sums):
    part = jnp.sum(sums.reshape(TAPS + 1, 8, 2, HD), axis=(1, 2))
    for bit in (1, 2, 4, 8):
        part = part + swap(part, "dp", bit)
    part = part + swap(part, "seq", HEADS)
    part = part[None]
    for bit in (1, 2, 4, 8):
        part = joined(part, "seq", bit)
    whole = jnp.moveaxis(part, 0, 1).reshape(TAPS + 1, HEADS * HD)
    return whole[:TAPS], whole[TAPS]


def on_device(
    queries, key_vectors, value_vectors, features, cotangent, frames, conv_kernel, conv_bias
):
    rows, utts, _ = queries.shape
    item = lax.axis_index("seq")
    utt = item // HEADS
    head = item % HEADS
    valid = jnp.sum(jnp.where(jnp.arange(utts) == utt, frames, 0), keepdims=True)
    taps = jnp.concatenate([conv_kernel, conv_bias[None]], axis=0)
    taps = lax.dynamic_slice_in_dim(taps, head * HD, HD, axis=1)
    taps = jnp.concatenate([taps, taps], axis=1)

    qkv = exchange(pack_qkv(queries, key_vectors, value_vectors))
    fc = exchange(pack_fc(features, cotangent))
    e, ctx = forward(valid, qkv)
    bogf, sums, gaug = conv(valid, fc, ctx, taps)
    bogf = exchange(bogf)
    grads = exchange(backward(qkv, gaug, e))
    grad_kernel, grad_bias = reduce_params(sums)
    block_out, grad_features = unpack(unpack_pair_kernel, bogf, rows, utts, 2)
    grad_q, grad_k, grad_v = unpack(unpack_qkv_kernel, grads, rows, utts, 3)
    return block_out, grad_features, grad_q, grad_k, grad_v, grad_kernel, grad_bias


def solution(mesh):
    field = P("seq", "dp", None)
    return jax.shard_map(
        on_device,
        mesh=mesh,
        in_specs=(field,) * 5 + (P("dp"), P(), P()),
        out_specs=(field,) * 5 + (P(), P()),
        check_vma=False,
    )
```

```python
import math

import jax
import jax.numpy as jnp
from jax import lax
from jax.experimental import pallas as pl
from jax.experimental.pallas import tpu as pltpu
from jax.sharding import PartitionSpec as P

HEADS = 16
TAPS = 31
HD = 64
LANES = 128
PAD = 16
QB = 1024
KC = 256
F32 = jnp.float32
BF16 = jnp.bfloat16
NEG = -1e30
LOG2E = math.log2(math.e)

VMEM = pl.BlockSpec(memory_space=pltpu.VMEM)
SMEM = pl.BlockSpec(memory_space=pltpu.SMEM)


def params(mib):
    return pltpu.CompilerParams(vmem_limit_bytes=mib * 1024 * 1024)


def lane_pair(low, high):
    return jnp.concatenate([low, high], axis=-1)


def swap_halves(x):
    return pltpu.roll(x, HD, x.ndim - 1)


def lane_ids(shape):
    return lax.broadcasted_iota(jnp.int32, shape, len(shape) - 1)


def pack_kernel(q_hbm, k_hbm, v_hbm, f_hbm, c_hbm, out_ref, q_ref, k_ref, v_ref, f_ref, c_ref, sems):
    pairs = ((q_hbm, q_ref), (k_hbm, k_ref), (v_hbm, v_ref), (f_hbm, f_ref), (c_hbm, c_ref))
    copies = [pltpu.make_async_copy(a, b, sems.at[n]) for n, (a, b) in enumerate(pairs)]
    for copy in copies:
        copy.start()
    rows, utts, _ = q_ref.shape

    def pair(a_ref, b_ref, first):
        for u in range(utts):
            a = a_ref[:, u, :]
            b = b_ref[:, u, :]
            for h in range(HEADS):
                part = slice(h * HD, (h + 1) * HD)
                out_ref[u * HEADS + h, first : first + rows, :] = lane_pair(a[:, part], b[:, part])

    copies[0].wait()
    copies[1].wait()
    pair(q_ref, k_ref, 0)
    copies[2].wait()
    for u in range(utts):
        v = v_ref[:, u, :]
        for h in range(HEADS):
            part = slice(h * HD, (h + 1) * HD)
            out_ref[u * HEADS + h, rows : rows * 3 // 2, :] = lane_pair(
                v[: rows // 2, part], v[rows // 2 :, part]
            )
    copies[3].wait()
    copies[4].wait()
    pair(f_ref, c_ref, rows * 3 // 2)


def unpack_kernel(in_ref, q_ref, k_ref, v_ref, f_ref, c_ref):
    rows, utts, _ = q_ref.shape

    def pair(a_ref, b_ref, first):
        firsts, seconds = [], []
        for u in range(utts):
            blocks = [in_ref[u * HEADS + h, first : first + rows, :] for h in range(HEADS)]
            firsts.append(jnp.concatenate([x[:, :HD] for x in blocks], axis=1))
            seconds.append(jnp.concatenate([x[:, HD:] for x in blocks], axis=1))
        a_ref[...] = jnp.stack(firsts, axis=1)
        b_ref[...] = jnp.stack(seconds, axis=1)

    pair(f_ref, c_ref, rows * 3 // 2)
    pair(q_ref, k_ref, 0)
    values = []
    for u in range(utts):
        blocks = [in_ref[u * HEADS + h, rows : rows * 3 // 2, :] for h in range(HEADS)]
        top = jnp.concatenate([x[:, :HD] for x in blocks], axis=1)
        bottom = jnp.concatenate([x[:, HD:] for x in blocks], axis=1)
        values.append(jnp.concatenate([top, bottom], axis=0))
    v_ref[...] = jnp.stack(values, axis=1)


def attend_forward(valid, in_ref, e_ref, ctx_ref, kaug, vaug, vt, kt, scores):
    sources = in_ref.shape[0]
    rows = in_ref.shape[1] * 2 // 5
    length = sources * rows
    per_block = QB // rows
    blocks = length // QB

    qk = in_ref[:, :rows, :].reshape(length, LANES).astype(F32)
    lane = lane_ids(qk.shape)
    position = lax.broadcasted_iota(jnp.int32, qk.shape, 0)
    bias = jnp.where(position < valid, 0.0, NEG)
    keys = jnp.where(lane < HD, swap_halves(qk), jnp.where(lane == HD, bias, 0.0))
    kaug[...] = keys.astype(BF16)
    half = in_ref[:, rows : rows * 3 // 2, :].astype(F32)
    swapped = swap_halves(half.reshape(length // 2, LANES)).reshape(half.shape)
    values = jnp.concatenate([half, swapped], axis=1).reshape(length, LANES)
    values = jnp.where(lane < HD, values, jnp.where(lane < HD + 2, 1.0, 0.0))
    vaug[...] = values.astype(BF16)
    vt[...] = values.T.astype(BF16)
    kt[...] = jnp.where(lane < HD, keys, 0.0).T.astype(BF16)

    def query_block(block):
        q = in_ref[pl.ds(block * per_block, per_block), :rows, :].reshape(QB, LANES).astype(F32)
        lane = lane_ids(q.shape)
        return jnp.where(lane < HD, q * 0.125, jnp.where(lane == HD, 1.0, 0.0)).astype(BF16)

    def score(slot, q, c):
        part = slice(c * KC, (c + 1) * KC)
        s = lax.dot_general(kaug[part, :], q, (((1,), (1,)), ((), ())), preferred_element_type=F32)
        scores[slot, part, :] = s
        return jnp.max(s, axis=0, keepdims=True)

    def weigh(block, slot, top, c):
        part = slice(c * KC, (c + 1) * KC)
        e = jnp.exp2((scores[slot, part, :] - top) * LOG2E).astype(BF16)
        e_ref[block, part, :] = e
        return jnp.dot(vt[:, part], e, preferred_element_type=F32)

    def finish(block, total):
        inverse = 1.0 / total[HD : HD + 1, :]
        row = lax.broadcasted_iota(jnp.int32, total.shape, 0)
        total = jnp.where(row < HD, total, 1.0) * inverse
        ctx_ref[pl.ds(pl.multiple_of(block * QB, QB), QB), :] = total.T

    chunks = range(length // KC)
    q = query_block(0)
    top = None
    for c in chunks:
        high = score(0, q, c)
        top = high if top is None else jnp.maximum(top, high)

    def step(block, top):
        slot = block % 2
        q = query_block(block + 1)
        total, later = None, None
        for c in chunks:
            high = score(1 - slot, q, c)
            term = weigh(block, slot, top, c)
            total = term if total is None else total + term
            later = high if later is None else jnp.maximum(later, high)
        finish(block, total)
        return later

    top = lax.fori_loop(0, blocks - 1, step, top)
    total = None
    for c in chunks:
        term = weigh(blocks - 1, (blocks - 1) % 2, top, c)
        total = term if total is None else total + term
    finish(blocks - 1, total)


def convolve(valid, in_ref, ctx_ref, taps_ref, out_ref, sums_ref, gaug_ref, field, grad, hid, cot, bo):
    sources = in_ref.shape[0]
    rows = in_ref.shape[1] * 2 // 5
    first = rows * 3 // 2
    length = sources * rows
    half = length // 2
    mid = sources // 2
    step = 64
    steps = half // step
    lane = lane_ids((half, LANES))
    fc_low = in_ref[:mid, first:, :].reshape(half, LANES).astype(F32)
    fc_high = in_ref[mid:, first:, :].reshape(half, LANES).astype(F32)
    features = jnp.where(lane < HD, fc_low, swap_halves(fc_high))
    cot[...] = jnp.where(lane < HD, swap_halves(fc_low), fc_high)
    ctx = jnp.where(lane < HD, ctx_ref[:half, :], swap_halves(ctx_ref[half:, :]))
    hidden = features + ctx.astype(BF16).astype(F32)
    hid[...] = hidden
    position = lax.broadcasted_iota(jnp.int32, (half, LANES), 0) + jnp.where(lane < HD, 0, half)
    masked = jnp.where(position < valid, hidden, 0.0).astype(BF16).astype(F32)
    small = lane_ids((PAD, LANES))
    field[PAD : PAD + half, :] = masked
    field[:PAD, :] = jnp.where(small < HD, 0.0, swap_halves(masked[half - PAD :, :]))
    field[PAD + half :, :] = jnp.where(small < HD, swap_halves(masked[:PAD, :]), 0.0)
    sums_ref[...] = jnp.zeros_like(sums_ref)
    bias = taps_ref[TAPS : TAPS + 1, :]

    def forward_step(i, carry):
        base = pl.multiple_of(i * step, step)
        out = jnp.broadcast_to(bias, (step, LANES))
        for k in range(TAPS):
            out = out + taps_ref[k : k + 1, :] * field[pl.ds(base + (k + 1), step), :]
        gate = 1.0 / (1.0 + jnp.exp(-out))
        bo[pl.ds(base, step), :] = hid[pl.ds(base, step), :] + out * gate
        g = cot[pl.ds(base, step), :] * gate * (1.0 + out * (1.0 - gate))
        grad[pl.ds(base + PAD, step), :] = g.astype(BF16).astype(F32)
        for k in range(TAPS):
            term = g * field[pl.ds(base + (k + 1), step), :]
            part = slice(8 * k, 8 * k + 8)
            sums_ref[part, :] += jnp.sum(term.reshape(step // 8, 8, LANES), axis=0)
        part = slice(8 * TAPS, 8 * TAPS + 8)
        sums_ref[part, :] += jnp.sum(g.reshape(step // 8, 8, LANES), axis=0)
        return carry

    lax.fori_loop(0, steps, forward_step, 0)
    grad[:PAD, :] = jnp.where(small < HD, 0.0, swap_halves(grad[half : half + PAD, :]))
    grad[PAD + half :, :] = jnp.where(small < HD, swap_halves(grad[PAD : 2 * PAD, :]), 0.0)
    lane_step = lane_ids((step, LANES))
    rows_step = lax.broadcasted_iota(jnp.int32, (step, LANES), 0)
    place = rows_step + jnp.where(lane_step < HD, 0, half)
    per_step = step // rows

    def augmented(gf, context):
        inverse = context[:, HD : HD + 1]
        gn = (gf * (inverse * 0.125)).astype(BF16).astype(F32)
        delta = jnp.sum(jnp.where(lane_step < HD, gn * context, 0.0), axis=1, keepdims=True)
        upper = delta.astype(BF16).astype(F32)
        tail = jnp.where(lane_step == HD, -upper, jnp.where(lane_step == HD + 1, upper - delta, 0.0))
        return jnp.where(lane_step < HD, gn, tail).astype(BF16)

    def backward_step(i, carry):
        base = pl.multiple_of(i * step, step)
        out = None
        for k in range(TAPS):
            term = taps_ref[k : k + 1, :] * grad[pl.ds(base + (TAPS - k), step), :]
            out = term if out is None else out + term
        out = jnp.where(place + base < valid, out, 0.0)
        gf = (cot[pl.ds(base, step), :] + out).astype(BF16).astype(F32)
        swapped = swap_halves(gf)
        block = bo[pl.ds(base, step), :]
        low = jnp.where(lane_step < HD, block, swapped).astype(BF16)
        high = jnp.where(lane_step < HD, swap_halves(block), gf).astype(BF16)
        at = i * per_step
        out_ref[pl.ds(at, per_step), first:, :] = low.reshape(per_step, rows, LANES)
        out_ref[pl.ds(mid + at, per_step), first:, :] = high.reshape(per_step, rows, LANES)
        gaug_ref[pl.ds(base, step), :] = augmented(gf, ctx_ref[pl.ds(base, step), :])
        other = pl.multiple_of(base + half, step)
        gaug_ref[pl.ds(other, step), :] = augmented(swapped, ctx_ref[pl.ds(other, step), :])
        return carry

    lax.fori_loop(0, steps, backward_step, 0)


def attend_backward(in_ref, e_ref, gaug_ref, out_ref, vaug, kt, acc):
    sources = in_ref.shape[0]
    rows = in_ref.shape[1] * 2 // 5
    length = sources * rows
    per_block = QB // rows
    chunks = length // KC
    acc[...] = jnp.zeros_like(acc)

    def step(block, carry):
        q = in_ref[pl.ds(block * per_block, per_block), :rows, :].reshape(QB, LANES).astype(F32)
        g = gaug_ref[pl.ds(pl.multiple_of(block * QB, QB), QB), :]
        lane = lane_ids(q.shape)
        right = jnp.where(lane < HD, 0.0, swap_halves(q)).astype(BF16)
        left = jnp.where(lane < HD, g.astype(F32), 0.0).astype(BF16)

        def spread(c):
            return lax.dot_general(
                vaug[c * KC : (c + 1) * KC, :],
                g,
                (((1,), (1,)), ((), ())),
                preferred_element_type=F32,
            )

        total = None
        dp = spread(0)
        for c in range(chunks):
            part = slice(c * KC, (c + 1) * KC)
            e = e_ref[block, part, :]
            ds = (e.astype(F32) * dp).astype(BF16)
            if c + 1 < chunks:
                dp = spread(c + 1)
            acc[part, :] += jnp.dot(e, left, preferred_element_type=F32) + jnp.dot(
                ds, right, preferred_element_type=F32
            )
            term = jnp.dot(kt[:, part], ds, preferred_element_type=F32)
            total = term if total is None else total + term
        at = pl.ds(block * per_block, per_block)
        out_ref[at, :rows, :] = total.T.astype(BF16).reshape(per_block, rows, LANES)
        return carry

    lax.fori_loop(0, length // QB, step, 0)
    both = acc[...].reshape(sources, rows, LANES)
    lane = lane_ids(both.shape)
    gq = out_ref[:, :rows, :].astype(F32)
    out_ref[:, :rows, :] = jnp.where(lane < HD, gq, both).astype(BF16)
    half = rows // 2
    upper = swap_halves(both[:, half:, :].reshape(length // 2, LANES)).reshape(sources, half, LANES)
    gv = jnp.where(lane_ids(upper.shape) < HD, both[:, :half, :], upper) * 8.0
    out_ref[:, rows : rows * 3 // 2, :] = gv.astype(BF16)


def item_kernel(
    frames_ref,
    in_ref,
    taps_ref,
    out_ref,
    sums_ref,
    e_ref,
    scores,
    ctx_ref,
    acc,
    kaug,
    vaug,
    vt,
    kt,
    gaug_ref,
    field,
    grad,
    hid,
    cot,
    bo,
):
    valid = frames_ref[0]
    attend_forward(valid, in_ref, e_ref, ctx_ref, kaug, vaug, vt, kt, scores)
    convolve(valid, in_ref, ctx_ref, taps_ref, out_ref, sums_ref, gaug_ref, field, grad, hid, cot, bo)
    attend_backward(in_ref, e_ref, gaug_ref, out_ref, vaug, kt, acc)


def shape_of(*dims, dtype=BF16):
    return jax.ShapeDtypeStruct(dims, dtype)


def pack(*fields):
    rows, utts, width = fields[0].shape
    return pl.pallas_call(
        pack_kernel,
        out_shape=shape_of(utts * HEADS, rows * 5 // 2, LANES),
        in_specs=[pl.BlockSpec(memory_space=pltpu.HBM)] * 5,
        out_specs=VMEM,
        scratch_shapes=[pltpu.VMEM((rows, utts, width), BF16)] * 5 + [pltpu.SemaphoreType.DMA((5,))],
        compiler_params=params(60),
        name="pack",
    )(*fields)


def unpack(field, rows, utts):
    return pl.pallas_call(
        unpack_kernel,
        out_shape=[shape_of(rows, utts, HEADS * HD)] * 5,
        in_specs=[VMEM],
        out_specs=[VMEM] * 5,
        compiler_params=params(24),
        name="unpack",
    )(field)


def item_step(frames, field, taps):
    sources, tall, _ = field.shape
    length = sources * (tall * 2 // 5)
    half = length // 2
    wide = (length, LANES)
    return pl.pallas_call(
        item_kernel,
        out_shape=[
            shape_of(sources, tall, LANES),
            shape_of(8 * (TAPS + 1), LANES, dtype=F32),
        ],
        in_specs=[SMEM, VMEM, VMEM],
        out_specs=[VMEM] * 2,
        scratch_shapes=[
            pltpu.VMEM((length // QB, length, QB), BF16),
            pltpu.VMEM((2, length, QB), F32),
            pltpu.VMEM(wide, F32),
            pltpu.VMEM(wide, F32),
            pltpu.VMEM(wide, BF16),
            pltpu.VMEM(wide, BF16),
            pltpu.VMEM((LANES, length), BF16),
            pltpu.VMEM((LANES, length), BF16),
            pltpu.VMEM(wide, BF16),
            pltpu.VMEM((half + 2 * PAD, LANES), F32),
            pltpu.VMEM((half + 2 * PAD, LANES), F32),
            pltpu.VMEM((half, LANES), F32),
            pltpu.VMEM((half, LANES), F32),
            pltpu.VMEM((half, LANES), F32),
        ],
        compiler_params=params(48),
        name="item_step",
    )(frames, field, taps)


def exchange(field):
    return lax.all_to_all(field, "seq", split_axis=0, concat_axis=0, tiled=True)


def swap(field, axis, bit):
    count = lax.axis_size(axis)
    return lax.ppermute(field, axis, [(i, i ^ bit) for i in range(count)])


def joined(field, axis, bit):
    other = swap(field, axis, bit)
    upper = (lax.axis_index(axis) & bit) != 0
    first = jnp.where(upper, other, field)
    second = jnp.where(upper, field, other)
    return jnp.concatenate([first, second], axis=0)


def reduce_params(sums):
    part = jnp.sum(sums.reshape(TAPS + 1, 8, 2, HD), axis=(1, 2))
    for bit in (4, 8):
        part = part + swap(part, "dp", bit)
    part = part + swap(part, "dp", 1) + swap(part, "dp", 2) + swap(part, "dp", 3)
    other = swap(part, "seq", 8) + swap(part, "seq", 24)
    part = part + swap(part, "seq", 16)
    upper = (lax.axis_index("seq") & 8) != 0
    part = jnp.stack([jnp.where(upper, other, part), jnp.where(upper, part, other)])[None]
    for bit in (1, 2, 4):
        part = joined(part, "seq", bit)
    whole = part.transpose(2, 1, 0, 3).reshape(TAPS + 1, HEADS * HD)
    return whole[:TAPS], whole[TAPS]


def on_device(
    queries, key_vectors, value_vectors, features, cotangent, frames, conv_kernel, conv_bias
):
    rows, utts, _ = queries.shape
    item = lax.axis_index("seq")
    utt = item // HEADS
    head = item % HEADS
    valid = jnp.sum(jnp.where(jnp.arange(utts) == utt, frames, 0), keepdims=True)
    taps = jnp.concatenate([conv_kernel, conv_bias[None]], axis=0)
    taps = lax.dynamic_slice_in_dim(taps, head * HD, HD, axis=1)
    taps = jnp.concatenate([taps, taps], axis=1)

    field = exchange(pack(queries, key_vectors, value_vectors, features, cotangent))
    field, sums = item_step(valid, field, taps)
    field = exchange(field)
    grad_kernel, grad_bias = reduce_params(sums)
    grad_q, grad_k, grad_v, block_out, grad_features = unpack(field, rows, utts)
    return block_out, grad_features, grad_q, grad_k, grad_v, grad_kernel, grad_bias


def solution(mesh):
    field = P("seq", "dp", None)
    return jax.shard_map(
        on_device,
        mesh=mesh,
        in_specs=(field,) * 5 + (P("dp"), P(), P()),
        out_specs=(field,) * 5 + (P(), P()),
        check_vma=False,
    )
```

```python
import math

import jax
import jax.numpy as jnp
from jax import lax
from jax.experimental import pallas as pl
from jax.experimental.pallas import tpu as pltpu
from jax.sharding import PartitionSpec as P

HEADS = 16
TAPS = 31
HD = 64
LANES = 128
PAD = 16
QB = 1024
KC = 256
F32 = jnp.float32
BF16 = jnp.bfloat16
NEG = -1e30
LOG2E = math.log2(math.e)

VMEM = pl.BlockSpec(memory_space=pltpu.VMEM)
SMEM = pl.BlockSpec(memory_space=pltpu.SMEM)


def params(mib):
    return pltpu.CompilerParams(vmem_limit_bytes=mib * 1024 * 1024)


def lane_pair(low, high):
    return jnp.concatenate([low, high], axis=-1)


def swap_halves(x):
    return pltpu.roll(x, HD, x.ndim - 1)


def lane_ids(shape):
    return lax.broadcasted_iota(jnp.int32, shape, len(shape) - 1)


def pack_kernel(q_hbm, k_hbm, v_hbm, f_hbm, c_hbm, out_ref, q_ref, k_ref, v_ref, f_ref, c_ref, sems):
    pairs = ((q_hbm, q_ref), (k_hbm, k_ref), (v_hbm, v_ref), (f_hbm, f_ref), (c_hbm, c_ref))
    copies = [pltpu.make_async_copy(a, b, sems.at[n]) for n, (a, b) in enumerate(pairs)]
    for copy in copies:
        copy.start()
    rows, utts, _ = q_ref.shape

    def pair(a_ref, b_ref, first):
        for u in range(utts):
            a = a_ref[:, u, :]
            b = b_ref[:, u, :]
            for h in range(HEADS):
                part = slice(h * HD, (h + 1) * HD)
                out_ref[u * HEADS + h, first : first + rows, :] = lane_pair(a[:, part], b[:, part])

    copies[0].wait()
    copies[1].wait()
    pair(q_ref, k_ref, 0)
    copies[2].wait()
    for u in range(utts):
        v = v_ref[:, u, :]
        for h in range(HEADS):
            part = slice(h * HD, (h + 1) * HD)
            out_ref[u * HEADS + h, rows : rows * 3 // 2, :] = lane_pair(
                v[: rows // 2, part], v[rows // 2 :, part]
            )
    copies[3].wait()
    copies[4].wait()
    pair(f_ref, c_ref, rows * 3 // 2)


def unpack_kernel(in_ref, q_ref, k_ref, v_ref, f_ref, c_ref):
    rows, utts, _ = q_ref.shape

    def pair(a_ref, b_ref, first):
        firsts, seconds = [], []
        for u in range(utts):
            blocks = [in_ref[u * HEADS + h, first : first + rows, :] for h in range(HEADS)]
            firsts.append(jnp.concatenate([x[:, :HD] for x in blocks], axis=1))
            seconds.append(jnp.concatenate([x[:, HD:] for x in blocks], axis=1))
        a_ref[...] = jnp.stack(firsts, axis=1)
        b_ref[...] = jnp.stack(seconds, axis=1)

    pair(f_ref, c_ref, rows * 3 // 2)
    pair(q_ref, k_ref, 0)
    values = []
    for u in range(utts):
        blocks = [in_ref[u * HEADS + h, rows : rows * 3 // 2, :] for h in range(HEADS)]
        top = jnp.concatenate([x[:, :HD] for x in blocks], axis=1)
        bottom = jnp.concatenate([x[:, HD:] for x in blocks], axis=1)
        values.append(jnp.concatenate([top, bottom], axis=0))
    v_ref[...] = jnp.stack(values, axis=1)


def attend_forward(valid, in_ref, e_ref, ctx_ref, kaug, vaug, vt, kt, scores):
    sources = in_ref.shape[0]
    rows = in_ref.shape[1] * 2 // 5
    length = sources * rows
    per_block = QB // rows
    blocks = length // QB

    qk = in_ref[:, :rows, :].reshape(length, LANES).astype(F32)
    lane = lane_ids(qk.shape)
    position = lax.broadcasted_iota(jnp.int32, qk.shape, 0)
    bias = jnp.where(position < valid, 0.0, NEG)
    keys = jnp.where(lane < HD, swap_halves(qk), jnp.where(lane == HD, bias, 0.0))
    kaug[...] = keys.astype(BF16)
    half = in_ref[:, rows : rows * 3 // 2, :].astype(F32)
    swapped = swap_halves(half.reshape(length // 2, LANES)).reshape(half.shape)
    values = jnp.concatenate([half, swapped], axis=1).reshape(length, LANES)
    values = jnp.where(lane < HD, values, jnp.where(lane < HD + 2, 1.0, 0.0))
    vaug[...] = values.astype(BF16)
    vt[...] = values.T.astype(BF16)
    kt[...] = jnp.where(lane < HD, keys, 0.0).T.astype(BF16)

    def query_block(block):
        q = in_ref[pl.ds(block * per_block, per_block), :rows, :].reshape(QB, LANES).astype(F32)
        lane = lane_ids(q.shape)
        return jnp.where(lane < HD, q * 0.125, jnp.where(lane == HD, 1.0, 0.0)).astype(BF16)

    def score(slot, q, c):
        part = slice(c * KC, (c + 1) * KC)
        s = lax.dot_general(kaug[part, :], q, (((1,), (1,)), ((), ())), preferred_element_type=F32)
        scores[slot, part, :] = s
        return jnp.max(s, axis=0, keepdims=True)

    def weigh(block, slot, top, c):
        part = slice(c * KC, (c + 1) * KC)
        e = jnp.exp2((scores[slot, part, :] - top) * LOG2E).astype(BF16)
        e_ref[block, part, :] = e
        return jnp.dot(vt[:, part], e, preferred_element_type=F32)

    def finish(block, total):
        inverse = 1.0 / total[HD : HD + 1, :]
        row = lax.broadcasted_iota(jnp.int32, total.shape, 0)
        total = jnp.where(row < HD, total, 1.0) * inverse
        ctx_ref[pl.ds(pl.multiple_of(block * QB, QB), QB), :] = total.T

    chunks = range(length // KC)
    q = query_block(0)
    top = None
    for c in chunks:
        high = score(0, q, c)
        top = high if top is None else jnp.maximum(top, high)

    def step(block, top):
        slot = block % 2
        q = query_block(block + 1)
        total, later = None, None
        for c in chunks:
            high = score(1 - slot, q, c)
            term = weigh(block, slot, top, c)
            total = term if total is None else total + term
            later = high if later is None else jnp.maximum(later, high)
        finish(block, total)
        return later

    top = lax.fori_loop(0, blocks - 1, step, top)
    total = None
    for c in chunks:
        term = weigh(blocks - 1, (blocks - 1) % 2, top, c)
        total = term if total is None else total + term
    finish(blocks - 1, total)


def convolve(
    valid, in_ref, ctx_ref, taps_ref, out_ref, part_ref, gaug_ref, field, grad, hid, cot, bo, sums_ref
):
    sources = in_ref.shape[0]
    rows = in_ref.shape[1] * 2 // 5
    first = rows * 3 // 2
    length = sources * rows
    half = length // 2
    mid = sources // 2
    step = 64
    steps = half // step
    lane = lane_ids((half, LANES))
    fc_low = in_ref[:mid, first:, :].reshape(half, LANES).astype(F32)
    fc_high = in_ref[mid:, first:, :].reshape(half, LANES).astype(F32)
    features = jnp.where(lane < HD, fc_low, swap_halves(fc_high))
    cot[...] = jnp.where(lane < HD, swap_halves(fc_low), fc_high)
    ctx = jnp.where(lane < HD, ctx_ref[:half, :], swap_halves(ctx_ref[half:, :]))
    hidden = features + ctx.astype(BF16).astype(F32)
    hid[...] = hidden
    position = lax.broadcasted_iota(jnp.int32, (half, LANES), 0) + jnp.where(lane < HD, 0, half)
    masked = jnp.where(position < valid, hidden, 0.0).astype(BF16).astype(F32)
    small = lane_ids((PAD, LANES))
    field[PAD : PAD + half, :] = masked
    field[:PAD, :] = jnp.where(small < HD, 0.0, swap_halves(masked[half - PAD :, :]))
    field[PAD + half :, :] = jnp.where(small < HD, swap_halves(masked[:PAD, :]), 0.0)
    sums_ref[...] = jnp.zeros_like(sums_ref)
    bias = taps_ref[TAPS : TAPS + 1, :]

    def forward_step(i, carry):
        base = pl.multiple_of(i * step, step)
        out = jnp.broadcast_to(bias, (step, LANES))
        for k in range(TAPS):
            out = out + taps_ref[k : k + 1, :] * field[pl.ds(base + (k + 1), step), :]
        gate = 1.0 / (1.0 + jnp.exp(-out))
        bo[pl.ds(base, step), :] = hid[pl.ds(base, step), :] + out * gate
        g = cot[pl.ds(base, step), :] * gate * (1.0 + out * (1.0 - gate))
        grad[pl.ds(base + PAD, step), :] = g.astype(BF16).astype(F32)
        for k in range(TAPS):
            term = g * field[pl.ds(base + (k + 1), step), :]
            part = slice(8 * k, 8 * k + 8)
            sums_ref[part, :] += jnp.sum(term.reshape(step // 8, 8, LANES), axis=0)
        part = slice(8 * TAPS, 8 * TAPS + 8)
        sums_ref[part, :] += jnp.sum(g.reshape(step // 8, 8, LANES), axis=0)
        return carry

    lax.fori_loop(0, steps, forward_step, 0)
    folded = jnp.sum(sums_ref[...].reshape(TAPS + 1, 8, LANES), axis=1)
    folded = folded + swap_halves(folded)
    taps_half = (TAPS + 1) // 2
    part_lane = lane_ids((taps_half, LANES))
    part_ref[...] = jnp.where(part_lane < HD, folded[:taps_half], folded[taps_half:])
    grad[:PAD, :] = jnp.where(small < HD, 0.0, swap_halves(grad[half : half + PAD, :]))
    grad[PAD + half :, :] = jnp.where(small < HD, swap_halves(grad[PAD : 2 * PAD, :]), 0.0)
    lane_step = lane_ids((step, LANES))
    rows_step = lax.broadcasted_iota(jnp.int32, (step, LANES), 0)
    place = rows_step + jnp.where(lane_step < HD, 0, half)
    per_step = step // rows

    def augmented(gf, context):
        inverse = context[:, HD : HD + 1]
        gn = (gf * (inverse * 0.125)).astype(BF16).astype(F32)
        delta = jnp.sum(jnp.where(lane_step < HD, gn * context, 0.0), axis=1, keepdims=True)
        upper = delta.astype(BF16).astype(F32)
        tail = jnp.where(lane_step == HD, -upper, jnp.where(lane_step == HD + 1, upper - delta, 0.0))
        return jnp.where(lane_step < HD, gn, tail).astype(BF16)

    def backward_step(i, carry):
        base = pl.multiple_of(i * step, step)
        out = None
        for k in range(TAPS):
            term = taps_ref[k : k + 1, :] * grad[pl.ds(base + (TAPS - k), step), :]
            out = term if out is None else out + term
        out = jnp.where(place + base < valid, out, 0.0)
        gf = (cot[pl.ds(base, step), :] + out).astype(BF16).astype(F32)
        swapped = swap_halves(gf)
        block = bo[pl.ds(base, step), :]
        low = jnp.where(lane_step < HD, block, swapped).astype(BF16)
        high = jnp.where(lane_step < HD, swap_halves(block), gf).astype(BF16)
        at = i * per_step
        out_ref[pl.ds(at, per_step), :, :] = low.reshape(per_step, rows, LANES)
        out_ref[pl.ds(mid + at, per_step), :, :] = high.reshape(per_step, rows, LANES)
        gaug_ref[pl.ds(base, step), :] = augmented(gf, ctx_ref[pl.ds(base, step), :])
        other = pl.multiple_of(base + half, step)
        gaug_ref[pl.ds(other, step), :] = augmented(swapped, ctx_ref[pl.ds(other, step), :])
        return carry

    lax.fori_loop(0, steps, backward_step, 0)


def backward_kernel(in_ref, e_ref, gaug_ref, vaug, kt, bogf_ref, out_ref, acc):
    sources = in_ref.shape[0]
    rows = in_ref.shape[1] * 2 // 5
    length = sources * rows
    per_block = QB // rows
    chunks = length // KC
    acc[...] = jnp.zeros_like(acc)
    out_ref[:, rows * 3 // 2 :, :] = bogf_ref[...]

    def step(block, carry):
        q = in_ref[pl.ds(block * per_block, per_block), :rows, :].reshape(QB, LANES).astype(F32)
        g = gaug_ref[pl.ds(pl.multiple_of(block * QB, QB), QB), :]
        lane = lane_ids(q.shape)
        right = jnp.where(lane < HD, 0.0, swap_halves(q)).astype(BF16)
        left = jnp.where(lane < HD, g.astype(F32), 0.0).astype(BF16)

        def spread(c):
            return lax.dot_general(
                vaug[c * KC : (c + 1) * KC, :],
                g,
                (((1,), (1,)), ((), ())),
                preferred_element_type=F32,
            )

        total = None
        dp = spread(0)
        for c in range(chunks):
            part = slice(c * KC, (c + 1) * KC)
            e = e_ref[block, part, :]
            ds = (e.astype(F32) * dp).astype(BF16)
            if c + 1 < chunks:
                dp = spread(c + 1)
            acc[part, :] += jnp.dot(e, left, preferred_element_type=F32) + jnp.dot(
                ds, right, preferred_element_type=F32
            )
            term = jnp.dot(kt[:, part], ds, preferred_element_type=F32)
            total = term if total is None else total + term
        at = pl.ds(block * per_block, per_block)
        out_ref[at, :rows, :] = total.T.astype(BF16).reshape(per_block, rows, LANES)
        return carry

    lax.fori_loop(0, length // QB, step, 0)
    both = acc[...].reshape(sources, rows, LANES)
    lane = lane_ids(both.shape)
    gq = out_ref[:, :rows, :].astype(F32)
    out_ref[:, :rows, :] = jnp.where(lane < HD, gq, both).astype(BF16)
    half = rows // 2
    upper = swap_halves(both[:, half:, :].reshape(length // 2, LANES)).reshape(sources, half, LANES)
    gv = jnp.where(lane_ids(upper.shape) < HD, both[:, :half, :], upper) * 8.0
    out_ref[:, rows : rows * 3 // 2, :] = gv.astype(BF16)


def forward_kernel(
    frames_ref,
    in_ref,
    taps_ref,
    e_ref,
    gaug_ref,
    vaug,
    kt,
    bogf_ref,
    part_ref,
    scores,
    ctx_ref,
    kaug,
    vt,
    field,
    grad,
    hid,
    cot,
    bo,
    sums_ref,
):
    valid = frames_ref[0]
    attend_forward(valid, in_ref, e_ref, ctx_ref, kaug, vaug, vt, kt, scores)
    convolve(
        valid, in_ref, ctx_ref, taps_ref, bogf_ref, part_ref, gaug_ref, field, grad, hid, cot, bo, sums_ref
    )


def params_kernel(in_ref, taps_ref, bias_ref):
    half = in_ref.shape[1]
    for h in range(0, HEADS, 2):
        part = slice(h * HD, (h + 2) * HD)
        a = in_ref[h]
        b = in_ref[h + 1]
        low = lane_pair(a[:, :HD], b[:, :HD])
        high = lane_pair(a[:, HD:], b[:, HD:])
        taps_ref[:half, part] = low
        taps_ref[half:, part] = high[: TAPS - half]
        bias_ref[:, part] = high[TAPS - half :]


def shape_of(*dims, dtype=BF16):
    return jax.ShapeDtypeStruct(dims, dtype)


def pack(*fields):
    rows, utts, width = fields[0].shape
    return pl.pallas_call(
        pack_kernel,
        out_shape=shape_of(utts * HEADS, rows * 5 // 2, LANES),
        in_specs=[pl.BlockSpec(memory_space=pltpu.HBM)] * 5,
        out_specs=VMEM,
        scratch_shapes=[pltpu.VMEM((rows, utts, width), BF16)] * 5 + [pltpu.SemaphoreType.DMA((5,))],
        compiler_params=params(60),
        name="pack",
    )(*fields)


def unpack(field, rows, utts):
    return pl.pallas_call(
        unpack_kernel,
        out_shape=[shape_of(rows, utts, HEADS * HD)] * 5,
        in_specs=[VMEM],
        out_specs=[VMEM] * 5,
        compiler_params=params(24),
        name="unpack",
    )(field)


def forward(frames, field, taps):
    sources, tall, _ = field.shape
    rows = tall * 2 // 5
    length = sources * rows
    half = length // 2
    wide = (length, LANES)
    return pl.pallas_call(
        forward_kernel,
        out_shape=[
            shape_of(length // QB, length, QB),
            shape_of(*wide),
            shape_of(*wide),
            shape_of(LANES, length),
            shape_of(sources, rows, LANES),
            shape_of((TAPS + 1) // 2, LANES, dtype=F32),
        ],
        in_specs=[SMEM, VMEM, VMEM],
        out_specs=[VMEM] * 6,
        scratch_shapes=[
            pltpu.VMEM((2, length, QB), F32),
            pltpu.VMEM(wide, F32),
            pltpu.VMEM(wide, BF16),
            pltpu.VMEM((LANES, length), BF16),
            pltpu.VMEM((half + 2 * PAD, LANES), F32),
            pltpu.VMEM((half + 2 * PAD, LANES), F32),
            pltpu.VMEM((half, LANES), F32),
            pltpu.VMEM((half, LANES), F32),
            pltpu.VMEM((half, LANES), F32),
            pltpu.VMEM((8 * (TAPS + 1), LANES), F32),
        ],
        compiler_params=params(36),
        cost_estimate=pl.CostEstimate(
            flops=8_000_000_000, bytes_accessed=20_000_000, transcendentals=4_000_000
        ),
        name="forward",
    )(frames, field, taps)


def backward(field, e, gaug, vaug, kt, bogf):
    length = e.shape[1]
    return pl.pallas_call(
        backward_kernel,
        out_shape=shape_of(*field.shape),
        in_specs=[VMEM] * 6,
        out_specs=VMEM,
        scratch_shapes=[pltpu.VMEM((length, LANES), F32)],
        compiler_params=params(36),
        cost_estimate=pl.CostEstimate(
            flops=9_000_000_000, bytes_accessed=20_000_000, transcendentals=0
        ),
        name="backward",
    )(field, e, gaug, vaug, kt, bogf)


def unpack_params(parts):
    width = HEADS * HD
    taps, bias = pl.pallas_call(
        params_kernel,
        out_shape=[shape_of(TAPS, width, dtype=F32), shape_of(1, width, dtype=F32)],
        in_specs=[VMEM],
        out_specs=[VMEM] * 2,
        compiler_params=params(8),
        name="unpack_params",
    )(parts)
    return taps, bias.reshape(width)


def exchange(field):
    return lax.all_to_all(field, "seq", split_axis=0, concat_axis=0, tiled=True)


def swap(field, axis, bit):
    count = lax.axis_size(axis)
    return lax.ppermute(field, axis, [(i, i ^ bit) for i in range(count)])


def joined(field, axis, bit):
    other = swap(field, axis, bit)
    upper = (lax.axis_index(axis) & bit) != 0
    first = jnp.where(upper, other, field)
    second = jnp.where(upper, field, other)
    return jnp.concatenate([first, second], axis=0)


def over_utterances(part):
    other = swap(part, "seq", 8) + swap(part, "seq", 24)
    part = part + swap(part, "seq", 16)
    upper = (lax.axis_index("seq") & 8) != 0
    return jnp.concatenate([jnp.where(upper, other, part), jnp.where(upper, part, other)], axis=0)


def over_devices(part):
    for bit in (4, 8):
        part = part + swap(part, "dp", bit)
    part = part + swap(part, "dp", 1) + swap(part, "dp", 2) + swap(part, "dp", 3)
    for bit in (1, 2, 4):
        part = joined(part, "seq", bit)
    half = (TAPS + 1) // 2
    part = part.reshape(HEADS // 2, 2, half, LANES).swapaxes(0, 1)
    return unpack_params(part.reshape(HEADS, half, LANES))


def on_device(
    queries, key_vectors, value_vectors, features, cotangent, frames, conv_kernel, conv_bias
):
    rows, utts, _ = queries.shape
    item = lax.axis_index("seq")
    utt = item // HEADS
    head = item % HEADS
    valid = jnp.sum(jnp.where(jnp.arange(utts) == utt, frames, 0), keepdims=True)
    taps = jnp.concatenate([conv_kernel, conv_bias[None]], axis=0)
    taps = lax.dynamic_slice_in_dim(taps, head * HD, HD, axis=1)
    taps = jnp.concatenate([taps, taps], axis=1)

    field = exchange(pack(queries, key_vectors, value_vectors, features, cotangent))
    *state, bogf, part = forward(valid, field, taps)
    part = over_utterances(part)
    field = backward(field, *state, bogf)
    field, part = lax.optimization_barrier((field, part))
    field = exchange(field)
    grad_kernel, grad_bias = over_devices(part)
    grad_q, grad_k, grad_v, block_out, grad_features = unpack(field, rows, utts)
    return block_out, grad_features, grad_q, grad_k, grad_v, grad_kernel, grad_bias


def solution(mesh):
    field = P("seq", "dp", None)
    return jax.shard_map(
        on_device,
        mesh=mesh,
        in_specs=(field,) * 5 + (P("dp"), P(), P()),
        out_specs=(field,) * 5 + (P(), P()),
        check_vma=False,
    )
```

```python
import math

import jax
import jax.numpy as jnp
from jax import lax
from jax.experimental import pallas as pl
from jax.experimental.pallas import tpu as pltpu
from jax.sharding import PartitionSpec as P

HEADS = 16
TAPS = 31
HD = 64
LANES = 128
PAD = 16
QB = 1024
KC = 256
F32 = jnp.float32
BF16 = jnp.bfloat16
NEG = -1e30
LOG2E = math.log2(math.e)

VMEM = pl.BlockSpec(memory_space=pltpu.VMEM)
SMEM = pl.BlockSpec(memory_space=pltpu.SMEM)


def params(mib):
    return pltpu.CompilerParams(vmem_limit_bytes=mib * 1024 * 1024)


def lane_pair(low, high):
    return jnp.concatenate([low, high], axis=-1)


def swap_halves(x):
    return pltpu.roll(x, HD, x.ndim - 1)


def lane_ids(shape):
    return lax.broadcasted_iota(jnp.int32, shape, len(shape) - 1)


def pack_kernel(q_hbm, k_hbm, v_hbm, f_hbm, c_hbm, out_ref, q_ref, k_ref, v_ref, f_ref, c_ref, sems):
    pairs = ((q_hbm, q_ref), (k_hbm, k_ref), (v_hbm, v_ref), (f_hbm, f_ref), (c_hbm, c_ref))
    copies = [pltpu.make_async_copy(a, b, sems.at[n]) for n, (a, b) in enumerate(pairs)]
    for copy in copies:
        copy.start()
    rows, utts, _ = q_ref.shape

    def pair(a_ref, b_ref, first):
        for u in range(utts):
            a = a_ref[:, u, :]
            b = b_ref[:, u, :]
            for h in range(HEADS):
                part = slice(h * HD, (h + 1) * HD)
                out_ref[u * HEADS + h, first : first + rows, :] = lane_pair(a[:, part], b[:, part])

    copies[0].wait()
    copies[1].wait()
    pair(q_ref, k_ref, 0)
    copies[2].wait()
    for u in range(utts):
        v = v_ref[:, u, :]
        for h in range(HEADS):
            part = slice(h * HD, (h + 1) * HD)
            out_ref[u * HEADS + h, rows : rows * 3 // 2, :] = lane_pair(
                v[: rows // 2, part], v[rows // 2 :, part]
            )
    copies[3].wait()
    copies[4].wait()
    pair(f_ref, c_ref, rows * 3 // 2)


def unpack_pair(in_ref, a_ref, b_ref):
    rows, utts, _ = a_ref.shape
    firsts, seconds = [], []
    for u in range(utts):
        blocks = [in_ref[u * HEADS + h, :rows, :] for h in range(HEADS)]
        firsts.append(jnp.concatenate([x[:, :HD] for x in blocks], axis=1))
        seconds.append(jnp.concatenate([x[:, HD:] for x in blocks], axis=1))
    a_ref[...] = jnp.stack(firsts, axis=1)
    b_ref[...] = jnp.stack(seconds, axis=1)


def unpack_qkv_kernel(in_ref, q_ref, k_ref, v_ref):
    unpack_pair(in_ref, q_ref, k_ref)
    rows, utts, _ = v_ref.shape
    values = []
    for u in range(utts):
        blocks = [in_ref[u * HEADS + h, rows:, :] for h in range(HEADS)]
        top = jnp.concatenate([x[:, :HD] for x in blocks], axis=1)
        bottom = jnp.concatenate([x[:, HD:] for x in blocks], axis=1)
        values.append(jnp.concatenate([top, bottom], axis=0))
    v_ref[...] = jnp.stack(values, axis=1)


def attend_forward(valid, in_ref, e_ref, ctx_ref, kaug, vaug, vt, kt, scores):
    sources = in_ref.shape[0]
    rows = in_ref.shape[1] * 2 // 5
    length = sources * rows
    per_block = QB // rows
    blocks = length // QB

    qk = in_ref[:, :rows, :].reshape(length, LANES).astype(F32)
    lane = lane_ids(qk.shape)
    position = lax.broadcasted_iota(jnp.int32, qk.shape, 0)
    bias = jnp.where(position < valid, 0.0, NEG)
    keys = jnp.where(lane < HD, swap_halves(qk), jnp.where(lane == HD, bias, 0.0))
    kaug[...] = keys.astype(BF16)
    half = in_ref[:, rows : rows * 3 // 2, :].astype(F32)
    swapped = swap_halves(half.reshape(length // 2, LANES)).reshape(half.shape)
    values = jnp.concatenate([half, swapped], axis=1).reshape(length, LANES)
    values = jnp.where(lane < HD, values, jnp.where(lane < HD + 2, 1.0, 0.0))
    vaug[...] = values.astype(BF16)
    vt[...] = values.T.astype(BF16)
    kt[...] = jnp.where(lane < HD, keys, 0.0).T.astype(BF16)

    def query_block(block):
        q = in_ref[pl.ds(block * per_block, per_block), :rows, :].reshape(QB, LANES).astype(F32)
        lane = lane_ids(q.shape)
        return jnp.where(lane < HD, q * 0.125, jnp.where(lane == HD, 1.0, 0.0)).astype(BF16)

    def score(slot, q, c):
        part = slice(c * KC, (c + 1) * KC)
        s = lax.dot_general(kaug[part, :], q, (((1,), (1,)), ((), ())), preferred_element_type=F32)
        scores[slot, part, :] = s
        return jnp.max(s, axis=0, keepdims=True)

    def weigh(block, slot, top, c):
        part = slice(c * KC, (c + 1) * KC)
        e = jnp.exp2((scores[slot, part, :] - top) * LOG2E).astype(BF16)
        e_ref[block, part, :] = e
        return jnp.dot(vt[:, part], e, preferred_element_type=F32)

    def finish(block, total):
        inverse = 1.0 / total[HD : HD + 1, :]
        row = lax.broadcasted_iota(jnp.int32, total.shape, 0)
        total = jnp.where(row < HD, total, 1.0) * inverse
        ctx_ref[pl.ds(pl.multiple_of(block * QB, QB), QB), :] = total.T

    chunks = range(length // KC)
    q = query_block(0)
    top = None
    for c in chunks:
        high = score(0, q, c)
        top = high if top is None else jnp.maximum(top, high)

    def step(block, top):
        slot = block % 2
        q = query_block(block + 1)
        total, later = None, None
        for c in chunks:
            high = score(1 - slot, q, c)
            term = weigh(block, slot, top, c)
            total = term if total is None else total + term
            later = high if later is None else jnp.maximum(later, high)
        finish(block, total)
        return later

    top = lax.fori_loop(0, blocks - 1, step, top)
    total = None
    for c in chunks:
        term = weigh(blocks - 1, (blocks - 1) % 2, top, c)
        total = term if total is None else total + term
    finish(blocks - 1, total)


def convolve(
    valid, in_ref, ctx_ref, taps_ref, out_ref, part_ref, gaug_ref, field, grad, hid, cot, bo, sums_ref
):
    sources = in_ref.shape[0]
    rows = in_ref.shape[1] * 2 // 5
    first = rows * 3 // 2
    length = sources * rows
    half = length // 2
    mid = sources // 2
    step = 64
    steps = half // step
    lane = lane_ids((half, LANES))
    fc_low = in_ref[:mid, first:, :].reshape(half, LANES).astype(F32)
    fc_high = in_ref[mid:, first:, :].reshape(half, LANES).astype(F32)
    features = jnp.where(lane < HD, fc_low, swap_halves(fc_high))
    cot[...] = jnp.where(lane < HD, swap_halves(fc_low), fc_high)
    ctx = jnp.where(lane < HD, ctx_ref[:half, :], swap_halves(ctx_ref[half:, :]))
    hidden = features + ctx.astype(BF16).astype(F32)
    hid[...] = hidden
    position = lax.broadcasted_iota(jnp.int32, (half, LANES), 0) + jnp.where(lane < HD, 0, half)
    masked = jnp.where(position < valid, hidden, 0.0).astype(BF16).astype(F32)
    small = lane_ids((PAD, LANES))
    field[PAD : PAD + half, :] = masked
    field[:PAD, :] = jnp.where(small < HD, 0.0, swap_halves(masked[half - PAD :, :]))
    field[PAD + half :, :] = jnp.where(small < HD, swap_halves(masked[:PAD, :]), 0.0)
    sums_ref[...] = jnp.zeros_like(sums_ref)
    bias = taps_ref[TAPS : TAPS + 1, :]

    def forward_step(i, carry):
        base = pl.multiple_of(i * step, step)
        out = jnp.broadcast_to(bias, (step, LANES))
        for k in range(TAPS):
            out = out + taps_ref[k : k + 1, :] * field[pl.ds(base + (k + 1), step), :]
        gate = 1.0 / (1.0 + jnp.exp(-out))
        bo[pl.ds(base, step), :] = hid[pl.ds(base, step), :] + out * gate
        g = cot[pl.ds(base, step), :] * gate * (1.0 + out * (1.0 - gate))
        grad[pl.ds(base + PAD, step), :] = g.astype(BF16).astype(F32)
        for k in range(TAPS):
            term = g * field[pl.ds(base + (k + 1), step), :]
            part = slice(8 * k, 8 * k + 8)
            sums_ref[part, :] += jnp.sum(term.reshape(step // 8, 8, LANES), axis=0)
        part = slice(8 * TAPS, 8 * TAPS + 8)
        sums_ref[part, :] += jnp.sum(g.reshape(step // 8, 8, LANES), axis=0)
        return carry

    lax.fori_loop(0, steps, forward_step, 0)
    folded = jnp.sum(sums_ref[...].reshape(TAPS + 1, 8, LANES), axis=1)
    folded = folded + swap_halves(folded)
    taps_half = (TAPS + 1) // 2
    part_lane = lane_ids((taps_half, LANES))
    part_ref[...] = jnp.where(part_lane < HD, folded[:taps_half], folded[taps_half:])
    grad[:PAD, :] = jnp.where(small < HD, 0.0, swap_halves(grad[half : half + PAD, :]))
    grad[PAD + half :, :] = jnp.where(small < HD, swap_halves(grad[PAD : 2 * PAD, :]), 0.0)
    lane_step = lane_ids((step, LANES))
    rows_step = lax.broadcasted_iota(jnp.int32, (step, LANES), 0)
    place = rows_step + jnp.where(lane_step < HD, 0, half)
    per_step = step // rows

    def augmented(gf, context):
        inverse = context[:, HD : HD + 1]
        gn = (gf * (inverse * 0.125)).astype(BF16).astype(F32)
        delta = jnp.sum(jnp.where(lane_step < HD, gn * context, 0.0), axis=1, keepdims=True)
        upper = delta.astype(BF16).astype(F32)
        tail = jnp.where(lane_step == HD, -upper, jnp.where(lane_step == HD + 1, upper - delta, 0.0))
        return jnp.where(lane_step < HD, gn, tail).astype(BF16)

    def backward_step(i, carry):
        base = pl.multiple_of(i * step, step)
        out = None
        for k in range(TAPS):
            term = taps_ref[k : k + 1, :] * grad[pl.ds(base + (TAPS - k), step), :]
            out = term if out is None else out + term
        out = jnp.where(place + base < valid, out, 0.0)
        gf = (cot[pl.ds(base, step), :] + out).astype(BF16).astype(F32)
        swapped = swap_halves(gf)
        block = bo[pl.ds(base, step), :]
        low = jnp.where(lane_step < HD, block, swapped).astype(BF16)
        high = jnp.where(lane_step < HD, swap_halves(block), gf).astype(BF16)
        at = i * per_step
        out_ref[pl.ds(at, per_step), :, :] = low.reshape(per_step, rows, LANES)
        out_ref[pl.ds(mid + at, per_step), :, :] = high.reshape(per_step, rows, LANES)
        gaug_ref[pl.ds(base, step), :] = augmented(gf, ctx_ref[pl.ds(base, step), :])
        other = pl.multiple_of(base + half, step)
        gaug_ref[pl.ds(other, step), :] = augmented(swapped, ctx_ref[pl.ds(other, step), :])
        return carry

    lax.fori_loop(0, steps, backward_step, 0)


def backward_kernel(in_ref, e_ref, gaug_ref, vaug, kt, out_ref, acc):
    sources = in_ref.shape[0]
    rows = in_ref.shape[1] * 2 // 5
    length = sources * rows
    per_block = QB // rows
    chunks = length // KC
    acc[...] = jnp.zeros_like(acc)

    def step(block, carry):
        q = in_ref[pl.ds(block * per_block, per_block), :rows, :].reshape(QB, LANES).astype(F32)
        g = gaug_ref[pl.ds(pl.multiple_of(block * QB, QB), QB), :]
        lane = lane_ids(q.shape)
        right = jnp.where(lane < HD, 0.0, swap_halves(q)).astype(BF16)
        left = jnp.where(lane < HD, g.astype(F32), 0.0).astype(BF16)

        def spread(c):
            return lax.dot_general(
                vaug[c * KC : (c + 1) * KC, :],
                g,
                (((1,), (1,)), ((), ())),
                preferred_element_type=F32,
            )

        total = None
        dp = spread(0)
        for c in range(chunks):
            part = slice(c * KC, (c + 1) * KC)
            e = e_ref[block, part, :]
            ds = (e.astype(F32) * dp).astype(BF16)
            if c + 1 < chunks:
                dp = spread(c + 1)
            acc[part, :] += jnp.dot(e, left, preferred_element_type=F32) + jnp.dot(
                ds, right, preferred_element_type=F32
            )
            term = jnp.dot(kt[:, part], ds, preferred_element_type=F32)
            total = term if total is None else total + term
        at = pl.ds(block * per_block, per_block)
        out_ref[at, :rows, :] = total.T.astype(BF16).reshape(per_block, rows, LANES)
        return carry

    lax.fori_loop(0, length // QB, step, 0)
    both = acc[...].reshape(sources, rows, LANES)
    lane = lane_ids(both.shape)
    gq = out_ref[:, :rows, :].astype(F32)
    out_ref[:, :rows, :] = jnp.where(lane < HD, gq, both).astype(BF16)
    half = rows // 2
    upper = swap_halves(both[:, half:, :].reshape(length // 2, LANES)).reshape(sources, half, LANES)
    gv = jnp.where(lane_ids(upper.shape) < HD, both[:, :half, :], upper) * 8.0
    out_ref[:, rows:, :] = gv.astype(BF16)


def forward_kernel(
    frames_ref,
    in_ref,
    taps_ref,
    e_ref,
    gaug_ref,
    vaug,
    kt,
    bogf_ref,
    part_ref,
    scores,
    ctx_ref,
    kaug,
    vt,
    field,
    grad,
    hid,
    cot,
    bo,
    sums_ref,
):
    valid = frames_ref[0]
    attend_forward(valid, in_ref, e_ref, ctx_ref, kaug, vaug, vt, kt, scores)
    convolve(
        valid, in_ref, ctx_ref, taps_ref, bogf_ref, part_ref, gaug_ref, field, grad, hid, cot, bo, sums_ref
    )


def params_kernel(in_ref, taps_ref, bias_ref):
    half = in_ref.shape[1]
    for h in range(0, HEADS, 2):
        part = slice(h * HD, (h + 2) * HD)
        a = in_ref[h]
        b = in_ref[h + 1]
        low = lane_pair(a[:, :HD], b[:, :HD])
        high = lane_pair(a[:, HD:], b[:, HD:])
        taps_ref[:half, part] = low
        taps_ref[half:, part] = high[: TAPS - half]
        bias_ref[:, part] = high[TAPS - half :]


def shape_of(*dims, dtype=BF16):
    return jax.ShapeDtypeStruct(dims, dtype)


def pack(*fields):
    rows, utts, width = fields[0].shape
    return pl.pallas_call(
        pack_kernel,
        out_shape=shape_of(utts * HEADS, rows * 5 // 2, LANES),
        in_specs=[pl.BlockSpec(memory_space=pltpu.HBM)] * 5,
        out_specs=VMEM,
        scratch_shapes=[pltpu.VMEM((rows, utts, width), BF16)] * 5 + [pltpu.SemaphoreType.DMA((5,))],
        compiler_params=params(60),
        name="pack",
    )(*fields)


def unpack(kernel, field, rows, utts, count):
    return pl.pallas_call(
        kernel,
        out_shape=[shape_of(rows, utts, HEADS * HD)] * count,
        in_specs=[VMEM],
        out_specs=[VMEM] * count,
        compiler_params=params(24),
        name="unpack%d" % count,
    )(field)


def forward(frames, field, taps):
    sources, tall, _ = field.shape
    rows = tall * 2 // 5
    length = sources * rows
    half = length // 2
    wide = (length, LANES)
    return pl.pallas_call(
        forward_kernel,
        out_shape=[
            shape_of(length // QB, length, QB),
            shape_of(*wide),
            shape_of(*wide),
            shape_of(LANES, length),
            shape_of(sources, rows, LANES),
            shape_of((TAPS + 1) // 2, LANES, dtype=F32),
        ],
        in_specs=[SMEM, VMEM, VMEM],
        out_specs=[VMEM] * 6,
        scratch_shapes=[
            pltpu.VMEM((2, length, QB), F32),
            pltpu.VMEM(wide, F32),
            pltpu.VMEM(wide, BF16),
            pltpu.VMEM((LANES, length), BF16),
            pltpu.VMEM((half + 2 * PAD, LANES), F32),
            pltpu.VMEM((half + 2 * PAD, LANES), F32),
            pltpu.VMEM((half, LANES), F32),
            pltpu.VMEM((half, LANES), F32),
            pltpu.VMEM((half, LANES), F32),
            pltpu.VMEM((8 * (TAPS + 1), LANES), F32),
        ],
        compiler_params=params(36),
        cost_estimate=pl.CostEstimate(
            flops=8_000_000_000, bytes_accessed=20_000_000, transcendentals=4_000_000
        ),
        name="forward",
    )(frames, field, taps)


def backward(field, e, gaug, vaug, kt):
    sources, tall, _ = field.shape
    length = e.shape[1]
    return pl.pallas_call(
        backward_kernel,
        out_shape=shape_of(sources, tall * 3 // 5, LANES),
        in_specs=[VMEM] * 5,
        out_specs=VMEM,
        scratch_shapes=[pltpu.VMEM((length, LANES), F32)],
        compiler_params=params(36),
        cost_estimate=pl.CostEstimate(
            flops=9_000_000_000, bytes_accessed=20_000_000, transcendentals=0
        ),
        name="backward",
    )(field, e, gaug, vaug, kt)


def unpack_params(parts):
    width = HEADS * HD
    taps, bias = pl.pallas_call(
        params_kernel,
        out_shape=[shape_of(TAPS, width, dtype=F32), shape_of(1, width, dtype=F32)],
        in_specs=[VMEM],
        out_specs=[VMEM] * 2,
        compiler_params=params(8),
        name="unpack_params",
    )(parts)
    return taps, bias.reshape(width)


def exchange(field):
    return lax.all_to_all(field, "seq", split_axis=0, concat_axis=0, tiled=True)


def swap(field, axis, bit):
    count = lax.axis_size(axis)
    return lax.ppermute(field, axis, [(i, i ^ bit) for i in range(count)])


def joined(field, axis, bit):
    other = swap(field, axis, bit)
    upper = (lax.axis_index(axis) & bit) != 0
    first = jnp.where(upper, other, field)
    second = jnp.where(upper, field, other)
    return jnp.concatenate([first, second], axis=0)


def over_y(part):
    for bit in (4, 8):
        part = part + swap(part, "dp", bit)
    return part


def over_z_low(part):
    return part + swap(part, "dp", 1) + swap(part, "dp", 2) + swap(part, "dp", 3)


def over_seq(part):
    other = swap(part, "seq", 8) + swap(part, "seq", 24)
    part = part + swap(part, "seq", 16)
    upper = (lax.axis_index("seq") & 8) != 0
    part = jnp.concatenate([jnp.where(upper, other, part), jnp.where(upper, part, other)], axis=0)
    for bit in (1, 2, 4):
        part = joined(part, "seq", bit)
    half = (TAPS + 1) // 2
    part = part.reshape(HEADS // 2, 2, half, LANES).swapaxes(0, 1)
    return unpack_params(part.reshape(HEADS, half, LANES))


def on_device(
    queries, key_vectors, value_vectors, features, cotangent, frames, conv_kernel, conv_bias
):
    rows, utts, _ = queries.shape
    item = lax.axis_index("seq")
    utt = item // HEADS
    head = item % HEADS
    valid = jnp.sum(jnp.where(jnp.arange(utts) == utt, frames, 0), keepdims=True)
    taps = jnp.concatenate([conv_kernel, conv_bias[None]], axis=0)
    taps = lax.dynamic_slice_in_dim(taps, head * HD, HD, axis=1)
    taps = jnp.concatenate([taps, taps], axis=1)

    field = exchange(pack(queries, key_vectors, value_vectors, features, cotangent))
    *state, bogf, part = forward(valid, field, taps)
    bogf = exchange(bogf)
    part = over_y(part)
    part = over_z_low(part)
    grads = backward(field, *state)
    grads, part = lax.optimization_barrier((grads, part))
    grads = exchange(grads)
    block_out, grad_features = unpack(unpack_pair, bogf, rows, utts, 2)
    grad_kernel, grad_bias = over_seq(part)
    grad_q, grad_k, grad_v = unpack(unpack_qkv_kernel, grads, rows, utts, 3)
    return block_out, grad_features, grad_q, grad_k, grad_v, grad_kernel, grad_bias


def solution(mesh):
    field = P("seq", "dp", None)
    return jax.shard_map(
        on_device,
        mesh=mesh,
        in_specs=(field,) * 5 + (P("dp"), P(), P()),
        out_specs=(field,) * 5 + (P(), P()),
        check_vma=False,
    )
```

```python
import math

import jax
import jax.numpy as jnp
from jax import lax
from jax.experimental import pallas as pl
from jax.experimental.pallas import tpu as pltpu
from jax.sharding import PartitionSpec as P

HEADS = 16
TAPS = 31
HD = 64
LANES = 128
PAD = 16
QB = 1024
KC = 256
F32 = jnp.float32
BF16 = jnp.bfloat16
NEG = -1e30
LOG2E = math.log2(math.e)

VMEM = pl.BlockSpec(memory_space=pltpu.VMEM)
SMEM = pl.BlockSpec(memory_space=pltpu.SMEM)


def params(mib):
    return pltpu.CompilerParams(vmem_limit_bytes=mib * 1024 * 1024)


def lane_pair(low, high):
    return jnp.concatenate([low, high], axis=-1)


def swap_halves(x):
    return pltpu.roll(x, HD, x.ndim - 1)


def lane_ids(shape):
    return lax.broadcasted_iota(jnp.int32, shape, len(shape) - 1)


def pack_kernel(q_hbm, k_hbm, v_hbm, f_hbm, c_hbm, out_ref, q_ref, k_ref, v_ref, f_ref, c_ref, sems):
    pairs = ((q_hbm, q_ref), (k_hbm, k_ref), (v_hbm, v_ref), (f_hbm, f_ref), (c_hbm, c_ref))
    copies = [pltpu.make_async_copy(a, b, sems.at[n]) for n, (a, b) in enumerate(pairs)]
    for copy in copies:
        copy.start()
    rows, utts, _ = q_ref.shape

    def pair(a_ref, b_ref, first):
        for u in range(utts):
            a = a_ref[:, u, :]
            b = b_ref[:, u, :]
            for h in range(HEADS):
                part = slice(h * HD, (h + 1) * HD)
                out_ref[u * HEADS + h, first : first + rows, :] = lane_pair(a[:, part], b[:, part])

    copies[0].wait()
    copies[1].wait()
    pair(q_ref, k_ref, 0)
    copies[2].wait()
    for u in range(utts):
        v = v_ref[:, u, :]
        for h in range(HEADS):
            part = slice(h * HD, (h + 1) * HD)
            out_ref[u * HEADS + h, rows : rows * 3 // 2, :] = lane_pair(
                v[: rows // 2, part], v[rows // 2 :, part]
            )
    copies[3].wait()
    copies[4].wait()
    pair(f_ref, c_ref, rows * 3 // 2)


def unpack_kernel(in_ref, q_ref, k_ref, v_ref, f_ref, c_ref):
    rows, utts, _ = q_ref.shape

    def pair(a_ref, b_ref, first):
        firsts, seconds = [], []
        for u in range(utts):
            blocks = [in_ref[u * HEADS + h, first : first + rows, :] for h in range(HEADS)]
            firsts.append(jnp.concatenate([x[:, :HD] for x in blocks], axis=1))
            seconds.append(jnp.concatenate([x[:, HD:] for x in blocks], axis=1))
        a_ref[...] = jnp.stack(firsts, axis=1)
        b_ref[...] = jnp.stack(seconds, axis=1)

    pair(f_ref, c_ref, rows * 3 // 2)
    pair(q_ref, k_ref, 0)
    values = []
    for u in range(utts):
        blocks = [in_ref[u * HEADS + h, rows : rows * 3 // 2, :] for h in range(HEADS)]
        top = jnp.concatenate([x[:, :HD] for x in blocks], axis=1)
        bottom = jnp.concatenate([x[:, HD:] for x in blocks], axis=1)
        values.append(jnp.concatenate([top, bottom], axis=0))
    v_ref[...] = jnp.stack(values, axis=1)


def attend_forward(valid, in_ref, e_ref, ctx_ref, kaug, vaug, vt, kt, scores):
    sources = in_ref.shape[0]
    rows = in_ref.shape[1] * 2 // 5
    length = sources * rows
    per_block = QB // rows
    blocks = length // QB

    qk = in_ref[:, :rows, :].reshape(length, LANES).astype(F32)
    lane = lane_ids(qk.shape)
    position = lax.broadcasted_iota(jnp.int32, qk.shape, 0)
    bias = jnp.where(position < valid, 0.0, NEG)
    keys = jnp.where(lane < HD, swap_halves(qk), jnp.where(lane == HD, bias, 0.0))
    kaug[...] = keys.astype(BF16)
    half = in_ref[:, rows : rows * 3 // 2, :].astype(F32)
    swapped = swap_halves(half.reshape(length // 2, LANES)).reshape(half.shape)
    values = jnp.concatenate([half, swapped], axis=1).reshape(length, LANES)
    values = jnp.where(lane < HD, values, jnp.where(lane < HD + 2, 1.0, 0.0))
    vaug[...] = values.astype(BF16)
    vt[...] = values.T.astype(BF16)
    kt[...] = jnp.where(lane < HD, keys, 0.0).T.astype(BF16)

    def query_block(block):
        q = in_ref[pl.ds(block * per_block, per_block), :rows, :].reshape(QB, LANES).astype(F32)
        lane = lane_ids(q.shape)
        return jnp.where(lane < HD, q * 0.125, jnp.where(lane == HD, 1.0, 0.0)).astype(BF16)

    def score(slot, q, c):
        part = slice(c * KC, (c + 1) * KC)
        s = lax.dot_general(kaug[part, :], q, (((1,), (1,)), ((), ())), preferred_element_type=F32)
        scores[slot, part, :] = s
        return jnp.max(s, axis=0, keepdims=True)

    def weigh(block, slot, top, c):
        part = slice(c * KC, (c + 1) * KC)
        e = jnp.exp2((scores[slot, part, :] - top) * LOG2E).astype(BF16)
        e_ref[block, part, :] = e
        return jnp.dot(vt[:, part], e, preferred_element_type=F32)

    def finish(block, total):
        inverse = 1.0 / total[HD : HD + 1, :]
        row = lax.broadcasted_iota(jnp.int32, total.shape, 0)
        total = jnp.where(row < HD, total, 1.0) * inverse
        ctx_ref[pl.ds(pl.multiple_of(block * QB, QB), QB), :] = total.T

    chunks = range(length // KC)
    q = query_block(0)
    top = None
    for c in chunks:
        high = score(0, q, c)
        top = high if top is None else jnp.maximum(top, high)

    def step(block, top):
        slot = block % 2
        q = query_block(block + 1)
        total, later = None, None
        for c in chunks:
            high = score(1 - slot, q, c)
            term = weigh(block, slot, top, c)
            total = term if total is None else total + term
            later = high if later is None else jnp.maximum(later, high)
        finish(block, total)
        return later

    top = lax.fori_loop(0, blocks - 1, step, top)
    total = None
    for c in chunks:
        term = weigh(blocks - 1, (blocks - 1) % 2, top, c)
        total = term if total is None else total + term
    finish(blocks - 1, total)


def convolve(
    valid, in_ref, ctx_ref, taps_ref, out_ref, part_ref, gaug_ref, field, grad, hid, cot, bo, sums_ref
):
    sources = in_ref.shape[0]
    rows = in_ref.shape[1] * 2 // 5
    first = rows * 3 // 2
    length = sources * rows
    half = length // 2
    mid = sources // 2
    step = 64
    steps = half // step
    lane = lane_ids((half, LANES))
    fc_low = in_ref[:mid, first:, :].reshape(half, LANES).astype(F32)
    fc_high = in_ref[mid:, first:, :].reshape(half, LANES).astype(F32)
    features = jnp.where(lane < HD, fc_low, swap_halves(fc_high))
    cot[...] = jnp.where(lane < HD, swap_halves(fc_low), fc_high)
    ctx = jnp.where(lane < HD, ctx_ref[:half, :], swap_halves(ctx_ref[half:, :]))
    hidden = features + ctx.astype(BF16).astype(F32)
    hid[...] = hidden
    position = lax.broadcasted_iota(jnp.int32, (half, LANES), 0) + jnp.where(lane < HD, 0, half)
    masked = jnp.where(position < valid, hidden, 0.0).astype(BF16).astype(F32)
    small = lane_ids((PAD, LANES))
    field[PAD : PAD + half, :] = masked
    field[:PAD, :] = jnp.where(small < HD, 0.0, swap_halves(masked[half - PAD :, :]))
    field[PAD + half :, :] = jnp.where(small < HD, swap_halves(masked[:PAD, :]), 0.0)
    sums_ref[...] = jnp.zeros_like(sums_ref)
    bias = taps_ref[TAPS : TAPS + 1, :]

    def forward_step(i, carry):
        base = pl.multiple_of(i * step, step)
        out = jnp.broadcast_to(bias, (step, LANES))
        for k in range(TAPS):
            out = out + taps_ref[k : k + 1, :] * field[pl.ds(base + (k + 1), step), :]
        gate = 1.0 / (1.0 + jnp.exp(-out))
        bo[pl.ds(base, step), :] = hid[pl.ds(base, step), :] + out * gate
        g = cot[pl.ds(base, step), :] * gate * (1.0 + out * (1.0 - gate))
        grad[pl.ds(base + PAD, step), :] = g.astype(BF16).astype(F32)
        for k in range(TAPS):
            term = g * field[pl.ds(base + (k + 1), step), :]
            part = slice(8 * k, 8 * k + 8)
            sums_ref[part, :] += jnp.sum(term.reshape(step // 8, 8, LANES), axis=0)
        part = slice(8 * TAPS, 8 * TAPS + 8)
        sums_ref[part, :] += jnp.sum(g.reshape(step // 8, 8, LANES), axis=0)
        return carry

    lax.fori_loop(0, steps, forward_step, 0)
    folded = jnp.sum(sums_ref[...].reshape(TAPS + 1, 8, LANES), axis=1)
    folded = folded + swap_halves(folded)
    taps_half = (TAPS + 1) // 2
    part_lane = lane_ids((taps_half, LANES))
    part_ref[...] = jnp.where(part_lane < HD, folded[:taps_half], folded[taps_half:])
    grad[:PAD, :] = jnp.where(small < HD, 0.0, swap_halves(grad[half : half + PAD, :]))
    grad[PAD + half :, :] = jnp.where(small < HD, swap_halves(grad[PAD : 2 * PAD, :]), 0.0)
    lane_step = lane_ids((step, LANES))
    rows_step = lax.broadcasted_iota(jnp.int32, (step, LANES), 0)
    place = rows_step + jnp.where(lane_step < HD, 0, half)
    per_step = step // rows

    def augmented(gf, context):
        inverse = context[:, HD : HD + 1]
        gn = (gf * (inverse * 0.125)).astype(BF16).astype(F32)
        delta = jnp.sum(jnp.where(lane_step < HD, gn * context, 0.0), axis=1, keepdims=True)
        upper = delta.astype(BF16).astype(F32)
        tail = jnp.where(lane_step == HD, -upper, jnp.where(lane_step == HD + 1, upper - delta, 0.0))
        return jnp.where(lane_step < HD, gn, tail).astype(BF16)

    def backward_step(i, carry):
        base = pl.multiple_of(i * step, step)
        out = None
        for k in range(TAPS):
            term = taps_ref[k : k + 1, :] * grad[pl.ds(base + (TAPS - k), step), :]
            out = term if out is None else out + term
        out = jnp.where(place + base < valid, out, 0.0)
        gf = (cot[pl.ds(base, step), :] + out).astype(BF16).astype(F32)
        swapped = swap_halves(gf)
        block = bo[pl.ds(base, step), :]
        low = jnp.where(lane_step < HD, block, swapped).astype(BF16)
        high = jnp.where(lane_step < HD, swap_halves(block), gf).astype(BF16)
        at = i * per_step
        out_ref[pl.ds(at, per_step), :, :] = low.reshape(per_step, rows, LANES)
        out_ref[pl.ds(mid + at, per_step), :, :] = high.reshape(per_step, rows, LANES)
        gaug_ref[pl.ds(base, step), :] = augmented(gf, ctx_ref[pl.ds(base, step), :])
        other = pl.multiple_of(base + half, step)
        gaug_ref[pl.ds(other, step), :] = augmented(swapped, ctx_ref[pl.ds(other, step), :])
        return carry

    lax.fori_loop(0, steps, backward_step, 0)


def backward_kernel(in_ref, e_ref, gaug_ref, vaug, kt, bogf_ref, out_ref, acc):
    sources = in_ref.shape[0]
    rows = in_ref.shape[1] * 2 // 5
    length = sources * rows
    per_block = QB // rows
    chunks = length // KC
    acc[...] = jnp.zeros_like(acc)
    out_ref[:, rows * 3 // 2 :, :] = bogf_ref[...]

    def step(block, carry):
        q = in_ref[pl.ds(block * per_block, per_block), :rows, :].reshape(QB, LANES).astype(F32)
        g = gaug_ref[pl.ds(pl.multiple_of(block * QB, QB), QB), :]
        lane = lane_ids(q.shape)
        right = jnp.where(lane < HD, 0.0, swap_halves(q)).astype(BF16)
        left = jnp.where(lane < HD, g.astype(F32), 0.0).astype(BF16)

        def spread(c):
            return lax.dot_general(
                vaug[c * KC : (c + 1) * KC, :],
                g,
                (((1,), (1,)), ((), ())),
                preferred_element_type=F32,
            )

        total = None
        dp = spread(0)
        for c in range(chunks):
            part = slice(c * KC, (c + 1) * KC)
            e = e_ref[block, part, :]
            ds = (e.astype(F32) * dp).astype(BF16)
            if c + 1 < chunks:
                dp = spread(c + 1)
            acc[part, :] += jnp.dot(e, left, preferred_element_type=F32) + jnp.dot(
                ds, right, preferred_element_type=F32
            )
            term = jnp.dot(kt[:, part], ds, preferred_element_type=F32)
            total = term if total is None else total + term
        at = pl.ds(block * per_block, per_block)
        out_ref[at, :rows, :] = total.T.astype(BF16).reshape(per_block, rows, LANES)
        return carry

    lax.fori_loop(0, length // QB, step, 0)
    both = acc[...].reshape(sources, rows, LANES)
    lane = lane_ids(both.shape)
    gq = out_ref[:, :rows, :].astype(F32)
    out_ref[:, :rows, :] = jnp.where(lane < HD, gq, both).astype(BF16)
    half = rows // 2
    upper = swap_halves(both[:, half:, :].reshape(length // 2, LANES)).reshape(sources, half, LANES)
    gv = jnp.where(lane_ids(upper.shape) < HD, both[:, :half, :], upper) * 8.0
    out_ref[:, rows : rows * 3 // 2, :] = gv.astype(BF16)


def forward_kernel(
    frames_ref,
    in_ref,
    taps_ref,
    e_ref,
    gaug_ref,
    vaug,
    kt,
    bogf_ref,
    part_ref,
    scores,
    ctx_ref,
    kaug,
    vt,
    field,
    grad,
    hid,
    cot,
    bo,
    sums_ref,
):
    valid = frames_ref[0]
    attend_forward(valid, in_ref, e_ref, ctx_ref, kaug, vaug, vt, kt, scores)
    convolve(
        valid, in_ref, ctx_ref, taps_ref, bogf_ref, part_ref, gaug_ref, field, grad, hid, cot, bo, sums_ref
    )


def params_kernel(place_ref, *refs):
    *parts, taps_ref, bias_ref, heads = refs
    place = place_ref[0]
    core, x, half = place % 2, place // 2 % len(parts), place // 8 % 2
    for i, part in enumerate(parts):
        for j in range(part.shape[0]):
            for n in range(part.shape[1]):
                other = (x + len(parts) - i) % len(parts)
                head = (half + n) % 2 * 8 + other * 2 + (core + j) % 2
                heads[head] = part[j, n]
    rows = heads.shape[1]
    for h in range(0, HEADS, 2):
        lanes = slice(h * HD, (h + 2) * HD)
        a = heads[h]
        b = heads[h + 1]
        low = lane_pair(a[:, :HD], b[:, :HD])
        high = lane_pair(a[:, HD:], b[:, HD:])
        taps_ref[:rows, lanes] = low
        taps_ref[rows:, lanes] = high[: TAPS - rows]
        bias_ref[:, lanes] = high[TAPS - rows :]


def shape_of(*dims, dtype=BF16):
    return jax.ShapeDtypeStruct(dims, dtype)


def pack(*fields):
    rows, utts, width = fields[0].shape
    return pl.pallas_call(
        pack_kernel,
        out_shape=shape_of(utts * HEADS, rows * 5 // 2, LANES),
        in_specs=[pl.BlockSpec(memory_space=pltpu.HBM)] * 5,
        out_specs=VMEM,
        scratch_shapes=[pltpu.VMEM((rows, utts, width), BF16)] * 5 + [pltpu.SemaphoreType.DMA((5,))],
        compiler_params=params(60),
        name="pack",
    )(*fields)


def unpack(field, rows, utts):
    return pl.pallas_call(
        unpack_kernel,
        out_shape=[shape_of(rows, utts, HEADS * HD)] * 5,
        in_specs=[VMEM],
        out_specs=[VMEM] * 5,
        compiler_params=params(24),
        name="unpack",
    )(field)


def forward(frames, field, taps):
    sources, tall, _ = field.shape
    rows = tall * 2 // 5
    length = sources * rows
    half = length // 2
    wide = (length, LANES)
    return pl.pallas_call(
        forward_kernel,
        out_shape=[
            shape_of(length // QB, length, QB),
            shape_of(*wide),
            shape_of(*wide),
            shape_of(LANES, length),
            shape_of(sources, rows, LANES),
            shape_of((TAPS + 1) // 2, LANES, dtype=F32),
        ],
        in_specs=[SMEM, VMEM, VMEM],
        out_specs=[VMEM] * 6,
        scratch_shapes=[
            pltpu.VMEM((2, length, QB), F32),
            pltpu.VMEM(wide, F32),
            pltpu.VMEM(wide, BF16),
            pltpu.VMEM((LANES, length), BF16),
            pltpu.VMEM((half + 2 * PAD, LANES), F32),
            pltpu.VMEM((half + 2 * PAD, LANES), F32),
            pltpu.VMEM((half, LANES), F32),
            pltpu.VMEM((half, LANES), F32),
            pltpu.VMEM((half, LANES), F32),
            pltpu.VMEM((8 * (TAPS + 1), LANES), F32),
        ],
        compiler_params=params(36),
        cost_estimate=pl.CostEstimate(
            flops=8_000_000_000, bytes_accessed=20_000_000, transcendentals=4_000_000
        ),
        name="forward",
    )(frames, field, taps)


def backward(field, e, gaug, vaug, kt, bogf):
    length = e.shape[1]
    return pl.pallas_call(
        backward_kernel,
        out_shape=shape_of(*field.shape),
        in_specs=[VMEM] * 6,
        out_specs=VMEM,
        scratch_shapes=[pltpu.VMEM((length, LANES), F32)],
        compiler_params=params(36),
        cost_estimate=pl.CostEstimate(
            flops=9_000_000_000, bytes_accessed=20_000_000, transcendentals=0
        ),
        name="backward",
    )(field, e, gaug, vaug, kt, bogf)


def unpack_params(place, parts):
    width = HEADS * HD
    taps, bias = pl.pallas_call(
        params_kernel,
        out_shape=[shape_of(TAPS, width, dtype=F32), shape_of(1, width, dtype=F32)],
        in_specs=[SMEM] + [VMEM] * len(parts),
        out_specs=[VMEM] * 2,
        scratch_shapes=[pltpu.VMEM((HEADS, *parts[0].shape[2:]), F32)],
        compiler_params=params(8),
        name="unpack_params",
    )(place.reshape(1), *parts)
    return taps, bias.reshape(width)


def exchange(field):
    return lax.all_to_all(field, "seq", split_axis=0, concat_axis=0, tiled=True)


def swap(field, axis, bit):
    count = lax.axis_size(axis)
    return lax.ppermute(field, axis, [(i, i ^ bit) for i in range(count)])


def along_x(field, steps):
    seq = lax.axis_size("seq")
    return lax.ppermute(field, "seq", [(i, i // 8 * 8 + (i + 2 * steps) % 8) for i in range(seq)])


def reduce_rest(part, place):
    for bit in (4, 8):
        part = part + swap(part, "dp", bit)
    other = swap(part, "seq", 8) + swap(part, "seq", 24)
    part = jnp.stack([part + swap(part, "seq", 16), other])
    part = jnp.stack([part, swap(part, "seq", 1)])
    return unpack_params(place, [part] + [along_x(part, steps) for steps in (1, 2, 3)])


def on_device(
    queries, key_vectors, value_vectors, features, cotangent, frames, conv_kernel, conv_bias
):
    rows, utts, _ = queries.shape
    item = lax.axis_index("seq")
    utt = item // HEADS
    head = item % HEADS
    valid = jnp.sum(jnp.where(jnp.arange(utts) == utt, frames, 0), keepdims=True)
    taps = jnp.concatenate([conv_kernel, conv_bias[None]], axis=0)
    taps = lax.dynamic_slice_in_dim(taps, head * HD, HD, axis=1)
    taps = jnp.concatenate([taps, taps], axis=1)

    field = exchange(pack(queries, key_vectors, value_vectors, features, cotangent))
    *state, bogf, part = forward(valid, field, taps)
    near = swap(part, "dp", 1)
    field = backward(field, *state, bogf)
    field, part, near = lax.optimization_barrier((field, part, near))
    part = part + near
    part = part + swap(part, "dp", 2)
    field, part = lax.optimization_barrier((field, part))
    field = exchange(field)
    grad_kernel, grad_bias = reduce_rest(part, item)
    grad_q, grad_k, grad_v, block_out, grad_features = unpack(field, rows, utts)
    return block_out, grad_features, grad_q, grad_k, grad_v, grad_kernel, grad_bias


def solution(mesh):
    field = P("seq", "dp", None)
    return jax.shard_map(
        on_device,
        mesh=mesh,
        in_specs=(field,) * 5 + (P("dp"), P(), P()),
        out_specs=(field,) * 5 + (P(), P()),
        check_vma=False,
    )
```

```python
import math

import jax
import jax.numpy as jnp
from jax import lax
from jax.experimental import pallas as pl
from jax.experimental.pallas import tpu as pltpu
from jax.sharding import PartitionSpec as P

HEADS = 16
TAPS = 31
HD = 64
LANES = 128
PAD = 16
QB = 1024
KC = 256
F32 = jnp.float32
BF16 = jnp.bfloat16
NEG = -1e30
LOG2E = math.log2(math.e)

VMEM = pl.BlockSpec(memory_space=pltpu.VMEM)
SMEM = pl.BlockSpec(memory_space=pltpu.SMEM)


def params(mib):
    return pltpu.CompilerParams(vmem_limit_bytes=mib * 1024 * 1024)


def lane_pair(low, high):
    return jnp.concatenate([low, high], axis=-1)


def swap_halves(x):
    return pltpu.roll(x, HD, x.ndim - 1)


def lane_ids(shape):
    return lax.broadcasted_iota(jnp.int32, shape, len(shape) - 1)


def pack_kernel(q_hbm, k_hbm, v_hbm, f_hbm, c_hbm, out_ref, q_ref, k_ref, v_ref, f_ref, c_ref, sems):
    pairs = ((q_hbm, q_ref), (k_hbm, k_ref), (v_hbm, v_ref), (f_hbm, f_ref), (c_hbm, c_ref))
    copies = [pltpu.make_async_copy(a, b, sems.at[n]) for n, (a, b) in enumerate(pairs)]
    for copy in copies:
        copy.start()
    rows, utts, width = q_ref.shape

    def one_head(field, u, h):
        return field[:, (u * HEADS + h) * HD : (u * HEADS + h + 1) * HD]

    def pair(a_ref, b_ref, first):
        a = a_ref[...].reshape(rows, utts * width)
        b = b_ref[...].reshape(rows, utts * width)
        for u in range(utts):
            for h in range(HEADS):
                out_ref[u * HEADS + h, first : first + rows, :] = lane_pair(
                    one_head(a, u, h), one_head(b, u, h)
                )

    copies[0].wait()
    copies[1].wait()
    pair(q_ref, k_ref, 0)
    copies[2].wait()
    values = v_ref[...].reshape(rows, utts * width)
    for u in range(utts):
        for h in range(HEADS):
            v = one_head(values, u, h)
            out_ref[u * HEADS + h, rows : rows * 3 // 2, :] = lane_pair(
                v[: rows // 2], v[rows // 2 :]
            )
    copies[3].wait()
    copies[4].wait()
    pair(f_ref, c_ref, rows * 3 // 2)


def unpack_kernel(in_ref, q_ref, k_ref, v_ref, f_ref, c_ref):
    rows, utts, _ = q_ref.shape

    def pair(a_ref, b_ref, first):
        firsts, seconds = [], []
        for u in range(utts):
            blocks = [in_ref[u * HEADS + h, first : first + rows, :] for h in range(HEADS)]
            firsts.append(jnp.concatenate([x[:, :HD] for x in blocks], axis=1))
            seconds.append(jnp.concatenate([x[:, HD:] for x in blocks], axis=1))
        a_ref[...] = jnp.concatenate(firsts, axis=1).reshape(a_ref.shape)
        b_ref[...] = jnp.concatenate(seconds, axis=1).reshape(b_ref.shape)

    pair(f_ref, c_ref, rows * 3 // 2)
    pair(q_ref, k_ref, 0)
    values = []
    for u in range(utts):
        blocks = [in_ref[u * HEADS + h, rows : rows * 3 // 2, :] for h in range(HEADS)]
        top = jnp.concatenate([x[:, :HD] for x in blocks], axis=1)
        bottom = jnp.concatenate([x[:, HD:] for x in blocks], axis=1)
        values.append(jnp.concatenate([top, bottom], axis=0))
    v_ref[...] = jnp.concatenate(values, axis=1).reshape(v_ref.shape)


def attend_forward(valid, in_ref, e_ref, ctx_ref, kaug, vaug, vt, kt, scores):
    sources = in_ref.shape[0]
    rows = in_ref.shape[1] * 2 // 5
    length = sources * rows
    per_block = QB // rows
    blocks = length // QB

    qk = in_ref[:, :rows, :].reshape(length, LANES).astype(F32)
    lane = lane_ids(qk.shape)
    position = lax.broadcasted_iota(jnp.int32, qk.shape, 0)
    bias = jnp.where(position < valid, 0.0, NEG)
    keys = jnp.where(lane < HD, swap_halves(qk), jnp.where(lane == HD, bias, 0.0))
    kaug[...] = keys.astype(BF16)
    half = in_ref[:, rows : rows * 3 // 2, :].astype(F32)
    swapped = swap_halves(half.reshape(length // 2, LANES)).reshape(half.shape)
    values = jnp.concatenate([half, swapped], axis=1).reshape(length, LANES)
    values = jnp.where(lane < HD, values, jnp.where(lane < HD + 2, 1.0, 0.0))
    vaug[...] = values.astype(BF16)
    vt[...] = values.T.astype(BF16)
    kt[...] = jnp.where(lane < HD, keys, 0.0).T.astype(BF16)

    def query_block(block):
        q = in_ref[pl.ds(block * per_block, per_block), :rows, :].reshape(QB, LANES).astype(F32)
        lane = lane_ids(q.shape)
        return jnp.where(lane < HD, q * 0.125, jnp.where(lane == HD, 1.0, 0.0)).astype(BF16)

    def score(slot, q, c):
        part = slice(c * KC, (c + 1) * KC)
        s = lax.dot_general(kaug[part, :], q, (((1,), (1,)), ((), ())), preferred_element_type=F32)
        scores[slot, part, :] = s
        return jnp.max(s, axis=0, keepdims=True)

    def weigh(block, slot, top, c):
        part = slice(c * KC, (c + 1) * KC)
        e = jnp.exp2((scores[slot, part, :] - top) * LOG2E).astype(BF16)
        e_ref[block, part, :] = e
        return jnp.dot(vt[:, part], e, preferred_element_type=F32)

    def finish(block, total):
        inverse = 1.0 / total[HD : HD + 1, :]
        row = lax.broadcasted_iota(jnp.int32, total.shape, 0)
        total = jnp.where(row < HD, total, 1.0) * inverse
        ctx_ref[pl.ds(pl.multiple_of(block * QB, QB), QB), :] = total.T

    chunks = range(length // KC)
    q = query_block(0)
    top = None
    for c in chunks:
        high = score(0, q, c)
        top = high if top is None else jnp.maximum(top, high)

    def step(block, top):
        slot = block % 2
        q = query_block(block + 1)
        total, later = None, None
        for c in chunks:
            high = score(1 - slot, q, c)
            term = weigh(block, slot, top, c)
            total = term if total is None else total + term
            later = high if later is None else jnp.maximum(later, high)
        finish(block, total)
        return later

    top = lax.fori_loop(0, blocks - 1, step, top)
    total = None
    for c in chunks:
        term = weigh(blocks - 1, (blocks - 1) % 2, top, c)
        total = term if total is None else total + term
    finish(blocks - 1, total)


def convolve(
    valid, in_ref, ctx_ref, taps_ref, out_ref, part_ref, gaug_ref, field, grad, hid, cot, bo, sums_ref
):
    sources = in_ref.shape[0]
    rows = in_ref.shape[1] * 2 // 5
    first = rows * 3 // 2
    length = sources * rows
    half = length // 2
    mid = sources // 2
    step = 64
    steps = half // step
    lane = lane_ids((half, LANES))
    fc_low = in_ref[:mid, first:, :].reshape(half, LANES).astype(F32)
    fc_high = in_ref[mid:, first:, :].reshape(half, LANES).astype(F32)
    features = jnp.where(lane < HD, fc_low, swap_halves(fc_high))
    cot[...] = jnp.where(lane < HD, swap_halves(fc_low), fc_high)
    ctx = jnp.where(lane < HD, ctx_ref[:half, :], swap_halves(ctx_ref[half:, :]))
    hidden = features + ctx.astype(BF16).astype(F32)
    hid[...] = hidden
    position = lax.broadcasted_iota(jnp.int32, (half, LANES), 0) + jnp.where(lane < HD, 0, half)
    masked = jnp.where(position < valid, hidden, 0.0).astype(BF16).astype(F32)
    small = lane_ids((PAD, LANES))
    field[PAD : PAD + half, :] = masked
    field[:PAD, :] = jnp.where(small < HD, 0.0, swap_halves(masked[half - PAD :, :]))
    field[PAD + half :, :] = jnp.where(small < HD, swap_halves(masked[:PAD, :]), 0.0)
    sums_ref[...] = jnp.zeros_like(sums_ref)
    bias = taps_ref[TAPS : TAPS + 1, :]

    def forward_step(i, carry):
        base = pl.multiple_of(i * step, step)
        out = jnp.broadcast_to(bias, (step, LANES))
        for k in range(TAPS):
            out = out + taps_ref[k : k + 1, :] * field[pl.ds(base + (k + 1), step), :]
        gate = 1.0 / (1.0 + jnp.exp(-out))
        bo[pl.ds(base, step), :] = hid[pl.ds(base, step), :] + out * gate
        g = cot[pl.ds(base, step), :] * gate * (1.0 + out * (1.0 - gate))
        grad[pl.ds(base + PAD, step), :] = g.astype(BF16).astype(F32)
        for k in range(TAPS):
            term = g * field[pl.ds(base + (k + 1), step), :]
            part = slice(8 * k, 8 * k + 8)
            sums_ref[part, :] += jnp.sum(term.reshape(step // 8, 8, LANES), axis=0)
        part = slice(8 * TAPS, 8 * TAPS + 8)
        sums_ref[part, :] += jnp.sum(g.reshape(step // 8, 8, LANES), axis=0)
        return carry

    lax.fori_loop(0, steps, forward_step, 0)
    folded = jnp.sum(sums_ref[...].reshape(TAPS + 1, 8, LANES), axis=1)
    folded = folded + swap_halves(folded)
    taps_half = (TAPS + 1) // 2
    part_lane = lane_ids((taps_half, LANES))
    part_ref[...] = jnp.where(part_lane < HD, folded[:taps_half], folded[taps_half:])
    grad[:PAD, :] = jnp.where(small < HD, 0.0, swap_halves(grad[half : half + PAD, :]))
    grad[PAD + half :, :] = jnp.where(small < HD, swap_halves(grad[PAD : 2 * PAD, :]), 0.0)
    lane_step = lane_ids((step, LANES))
    rows_step = lax.broadcasted_iota(jnp.int32, (step, LANES), 0)
    place = rows_step + jnp.where(lane_step < HD, 0, half)
    per_step = step // rows

    def augmented(gf, context):
        inverse = context[:, HD : HD + 1]
        gn = (gf * (inverse * 0.125)).astype(BF16).astype(F32)
        delta = jnp.sum(jnp.where(lane_step < HD, gn * context, 0.0), axis=1, keepdims=True)
        upper = delta.astype(BF16).astype(F32)
        tail = jnp.where(lane_step == HD, -upper, jnp.where(lane_step == HD + 1, upper - delta, 0.0))
        return jnp.where(lane_step < HD, gn, tail).astype(BF16)

    def backward_step(i, carry):
        base = pl.multiple_of(i * step, step)
        out = None
        for k in range(TAPS):
            term = taps_ref[k : k + 1, :] * grad[pl.ds(base + (TAPS - k), step), :]
            out = term if out is None else out + term
        out = jnp.where(place + base < valid, out, 0.0)
        gf = (cot[pl.ds(base, step), :] + out).astype(BF16).astype(F32)
        swapped = swap_halves(gf)
        block = bo[pl.ds(base, step), :]
        low = jnp.where(lane_step < HD, block, swapped).astype(BF16)
        high = jnp.where(lane_step < HD, swap_halves(block), gf).astype(BF16)
        at = i * per_step
        out_ref[pl.ds(at, per_step), :, :] = low.reshape(per_step, rows, LANES)
        out_ref[pl.ds(mid + at, per_step), :, :] = high.reshape(per_step, rows, LANES)
        gaug_ref[pl.ds(base, step), :] = augmented(gf, ctx_ref[pl.ds(base, step), :])
        other = pl.multiple_of(base + half, step)
        gaug_ref[pl.ds(other, step), :] = augmented(swapped, ctx_ref[pl.ds(other, step), :])
        return carry

    lax.fori_loop(0, steps, backward_step, 0)


def backward_kernel(in_ref, e_ref, gaug_ref, vaug, kt, bogf_ref, out_ref, acc):
    sources = in_ref.shape[0]
    rows = in_ref.shape[1] * 2 // 5
    length = sources * rows
    per_block = QB // rows
    chunks = length // KC
    acc[...] = jnp.zeros_like(acc)
    out_ref[:, rows * 3 // 2 :, :] = bogf_ref[...]

    def step(block, carry):
        q = in_ref[pl.ds(block * per_block, per_block), :rows, :].reshape(QB, LANES).astype(F32)
        g = gaug_ref[pl.ds(pl.multiple_of(block * QB, QB), QB), :]
        lane = lane_ids(q.shape)
        right = jnp.where(lane < HD, 0.0, swap_halves(q)).astype(BF16)
        left = jnp.where(lane < HD, g.astype(F32), 0.0).astype(BF16)

        def spread(c):
            return lax.dot_general(
                vaug[c * KC : (c + 1) * KC, :],
                g,
                (((1,), (1,)), ((), ())),
                preferred_element_type=F32,
            )

        total = None
        dp = spread(0)
        for c in range(chunks):
            part = slice(c * KC, (c + 1) * KC)
            e = e_ref[block, part, :]
            ds = (e.astype(F32) * dp).astype(BF16)
            if c + 1 < chunks:
                dp = spread(c + 1)
            acc[part, :] += jnp.dot(e, left, preferred_element_type=F32) + jnp.dot(
                ds, right, preferred_element_type=F32
            )
            term = jnp.dot(kt[:, part], ds, preferred_element_type=F32)
            total = term if total is None else total + term
        at = pl.ds(block * per_block, per_block)
        out_ref[at, :rows, :] = total.T.astype(BF16).reshape(per_block, rows, LANES)
        return carry

    lax.fori_loop(0, length // QB, step, 0)
    both = acc[...].reshape(sources, rows, LANES)
    lane = lane_ids(both.shape)
    gq = out_ref[:, :rows, :].astype(F32)
    out_ref[:, :rows, :] = jnp.where(lane < HD, gq, both).astype(BF16)
    half = rows // 2
    upper = swap_halves(both[:, half:, :].reshape(length // 2, LANES)).reshape(sources, half, LANES)
    gv = jnp.where(lane_ids(upper.shape) < HD, both[:, :half, :], upper) * 8.0
    out_ref[:, rows : rows * 3 // 2, :] = gv.astype(BF16)


def forward_kernel(
    frames_ref,
    in_ref,
    taps_ref,
    e_ref,
    gaug_ref,
    vaug,
    kt,
    bogf_ref,
    part_ref,
    scores,
    ctx_ref,
    kaug,
    vt,
    field,
    grad,
    hid,
    cot,
    bo,
    sums_ref,
):
    valid = frames_ref[0]
    attend_forward(valid, in_ref, e_ref, ctx_ref, kaug, vaug, vt, kt, scores)
    convolve(
        valid, in_ref, ctx_ref, taps_ref, bogf_ref, part_ref, gaug_ref, field, grad, hid, cot, bo, sums_ref
    )


def params_kernel(place_ref, same_ref, other_ref, taps_ref, bias_ref, heads):
    place = place_ref[0]
    core, x, half = place % 2, place // 2 % 4, place // 8 % 2
    for n, part in enumerate((same_ref, other_ref)):
        for i in range(part.shape[0]):
            for j in range(part.shape[1]):
                head = (half + n) % 2 * 8 + (x + 4 - i) % 4 * 2 + (core + j) % 2
                heads[head] = part[i, j]
    rows = heads.shape[1]
    for h in range(0, HEADS, 2):
        lanes = slice(h * HD, (h + 2) * HD)
        a = heads[h]
        b = heads[h + 1]
        low = lane_pair(a[:, :HD], b[:, :HD])
        high = lane_pair(a[:, HD:], b[:, HD:])
        taps_ref[:rows, lanes] = low
        taps_ref[rows:, lanes] = high[: TAPS - rows]
        bias_ref[:, lanes] = high[TAPS - rows :]


def shape_of(*dims, dtype=BF16):
    return jax.ShapeDtypeStruct(dims, dtype)


def pack(*fields):
    rows, utts, width = fields[0].shape
    return pl.pallas_call(
        pack_kernel,
        out_shape=shape_of(utts * HEADS, rows * 5 // 2, LANES),
        in_specs=[pl.BlockSpec(memory_space=pltpu.HBM)] * 5,
        out_specs=VMEM,
        scratch_shapes=[pltpu.VMEM((rows, utts, width), BF16)] * 5 + [pltpu.SemaphoreType.DMA((5,))],
        compiler_params=params(60),
        name="pack",
    )(*fields)


def unpack(field, rows, utts):
    return pl.pallas_call(
        unpack_kernel,
        out_shape=[shape_of(rows, utts, HEADS * HD)] * 5,
        in_specs=[VMEM],
        out_specs=[VMEM] * 5,
        compiler_params=params(24),
        name="unpack",
    )(field)


def forward(frames, field, taps):
    sources, tall, _ = field.shape
    rows = tall * 2 // 5
    length = sources * rows
    half = length // 2
    wide = (length, LANES)
    return pl.pallas_call(
        forward_kernel,
        out_shape=[
            shape_of(length // QB, length, QB),
            shape_of(*wide),
            shape_of(*wide),
            shape_of(LANES, length),
            shape_of(sources, rows, LANES),
            shape_of((TAPS + 1) // 2, LANES, dtype=F32),
        ],
        in_specs=[SMEM, VMEM, VMEM],
        out_specs=[VMEM] * 6,
        scratch_shapes=[
            pltpu.VMEM((2, length, QB), F32),
            pltpu.VMEM(wide, F32),
            pltpu.VMEM(wide, BF16),
            pltpu.VMEM((LANES, length), BF16),
            pltpu.VMEM((half + 2 * PAD, LANES), F32),
            pltpu.VMEM((half + 2 * PAD, LANES), F32),
            pltpu.VMEM((half, LANES), F32),
            pltpu.VMEM((half, LANES), F32),
            pltpu.VMEM((half, LANES), F32),
            pltpu.VMEM((8 * (TAPS + 1), LANES), F32),
        ],
        compiler_params=params(36),
        cost_estimate=pl.CostEstimate(
            flops=8_000_000_000, bytes_accessed=20_000_000, transcendentals=4_000_000
        ),
        name="forward",
    )(frames, field, taps)


def backward(field, e, gaug, vaug, kt, bogf):
    length = e.shape[1]
    return pl.pallas_call(
        backward_kernel,
        out_shape=shape_of(*field.shape),
        in_specs=[VMEM] * 6,
        out_specs=VMEM,
        scratch_shapes=[pltpu.VMEM((length, LANES), F32)],
        compiler_params=params(36),
        cost_estimate=pl.CostEstimate(
            flops=9_000_000_000, bytes_accessed=20_000_000, transcendentals=0
        ),
        name="backward",
    )(field, e, gaug, vaug, kt, bogf)


def unpack_params(place, parts):
    width = HEADS * HD
    taps, bias = pl.pallas_call(
        params_kernel,
        out_shape=[shape_of(TAPS, width, dtype=F32), shape_of(1, width, dtype=F32)],
        in_specs=[SMEM] + [VMEM] * len(parts),
        out_specs=[VMEM] * 2,
        scratch_shapes=[pltpu.VMEM((HEADS, *parts[0].shape[2:]), F32)],
        compiler_params=params(8),
        name="unpack_params",
    )(place.reshape(1), *parts)
    return taps, bias.reshape(width)


def exchange(field):
    return lax.all_to_all(field, "seq", split_axis=0, concat_axis=0, tiled=True)


def swap(field, axis, bit):
    count = lax.axis_size(axis)
    return lax.ppermute(field, axis, [(i, i ^ bit) for i in range(count)])


def along_x(field, steps):
    seq = lax.axis_size("seq")
    return lax.ppermute(field, "seq", [(i, i // 8 * 8 + (i + 2 * steps) % 8) for i in range(seq)])


def reduce_rest(part, place):
    for bit in (4, 8):
        part = part + swap(part, "dp", bit)
    part = jnp.stack([part, swap(part, "seq", 1)])
    part = jnp.stack([part] + [along_x(part, steps) for steps in (1, 2, 3)]).astype(BF16)
    wide = part.astype(F32)
    same = wide + swap(part, "seq", 16).astype(F32)
    other = swap(part, "seq", 8).astype(F32) + swap(part, "seq", 24).astype(F32)
    return unpack_params(place, [same, other])


def on_device(
    queries, key_vectors, value_vectors, features, cotangent, frames, conv_kernel, conv_bias
):
    rows, utts, _ = queries.shape
    item = lax.axis_index("seq")
    utt = item // HEADS
    head = item % HEADS
    valid = jnp.sum(jnp.where(jnp.arange(utts) == utt, frames, 0), keepdims=True)
    taps = jnp.concatenate([conv_kernel, conv_bias[None]], axis=0)
    taps = lax.dynamic_slice_in_dim(taps, head * HD, HD, axis=1)
    taps = jnp.concatenate([taps, taps], axis=1)

    field = exchange(pack(queries, key_vectors, value_vectors, features, cotangent))
    *state, bogf, part = forward(valid, field, taps)
    near = swap(part, "dp", 1)
    field = backward(field, *state, bogf)
    field, part, near = lax.optimization_barrier((field, part, near))
    part = part + near
    part = part + swap(part, "dp", 2)
    field, part = lax.optimization_barrier((field, part))
    field = exchange(field)
    grad_kernel, grad_bias = reduce_rest(part, item)
    grad_q, grad_k, grad_v, block_out, grad_features = unpack(field, rows, utts)
    return block_out, grad_features, grad_q, grad_k, grad_v, grad_kernel, grad_bias


def solution(mesh):
    field = P("seq", "dp", None)
    return jax.shard_map(
        on_device,
        mesh=mesh,
        in_specs=(field,) * 5 + (P("dp"), P(), P()),
        out_specs=(field,) * 5 + (P(), P()),
        check_vma=False,
    )
```

```python
import math

import jax
import jax.numpy as jnp
from jax import lax
from jax.experimental import pallas as pl
from jax.experimental.pallas import tpu as pltpu
from jax.sharding import PartitionSpec as P

HEADS = 16
TAPS = 31
HD = 64
LANES = 128
PAD = 16
QB = 1024
KC = 256
CONV_ROWS = 256
F32 = jnp.float32
BF16 = jnp.bfloat16
NEG = -1e30
LOG2E = math.log2(math.e)

VMEM = pl.BlockSpec(memory_space=pltpu.VMEM)
SMEM = pl.BlockSpec(memory_space=pltpu.SMEM)


def params(mib):
    return pltpu.CompilerParams(vmem_limit_bytes=mib * 1024 * 1024)


def lane_pair(low, high):
    return jnp.concatenate([low, high], axis=-1)


def swap_halves(x):
    return pltpu.roll(x, HD, x.ndim - 1)


def lane_ids(shape):
    return lax.broadcasted_iota(jnp.int32, shape, len(shape) - 1)


def pack_kernel(q_hbm, k_hbm, v_hbm, f_hbm, c_hbm, out_ref, q_ref, k_ref, v_ref, f_ref, c_ref, sems):
    pairs = ((q_hbm, q_ref), (k_hbm, k_ref), (v_hbm, v_ref), (f_hbm, f_ref), (c_hbm, c_ref))
    copies = [pltpu.make_async_copy(a, b, sems.at[n]) for n, (a, b) in enumerate(pairs)]
    for copy in copies:
        copy.start()
    rows, utts, width = q_ref.shape

    def one_head(field, u, h):
        return field[:, (u * HEADS + h) * HD : (u * HEADS + h + 1) * HD]

    def pair(a_ref, b_ref, first):
        a = a_ref[...].reshape(rows, utts * width)
        b = b_ref[...].reshape(rows, utts * width)
        for u in range(utts):
            for h in range(HEADS):
                out_ref[u * HEADS + h, first : first + rows, :] = lane_pair(
                    one_head(a, u, h), one_head(b, u, h)
                )

    copies[0].wait()
    copies[1].wait()
    pair(q_ref, k_ref, 0)
    copies[2].wait()
    values = v_ref[...].reshape(rows, utts * width)
    for u in range(utts):
        for h in range(HEADS):
            v = one_head(values, u, h)
            out_ref[u * HEADS + h, rows : rows * 3 // 2, :] = lane_pair(
                v[: rows // 2], v[rows // 2 :]
            )
    copies[3].wait()
    copies[4].wait()
    pair(f_ref, c_ref, rows * 3 // 2)


def unpack_kernel(in_ref, q_ref, k_ref, v_ref, f_ref, c_ref):
    rows, utts, _ = q_ref.shape

    def pair(a_ref, b_ref, first):
        firsts, seconds = [], []
        for u in range(utts):
            blocks = [in_ref[u * HEADS + h, first : first + rows, :] for h in range(HEADS)]
            firsts.append(jnp.concatenate([x[:, :HD] for x in blocks], axis=1))
            seconds.append(jnp.concatenate([x[:, HD:] for x in blocks], axis=1))
        a_ref[...] = jnp.concatenate(firsts, axis=1).reshape(a_ref.shape)
        b_ref[...] = jnp.concatenate(seconds, axis=1).reshape(b_ref.shape)

    pair(f_ref, c_ref, rows * 3 // 2)
    pair(q_ref, k_ref, 0)
    values = []
    for u in range(utts):
        blocks = [in_ref[u * HEADS + h, rows : rows * 3 // 2, :] for h in range(HEADS)]
        top = jnp.concatenate([x[:, :HD] for x in blocks], axis=1)
        bottom = jnp.concatenate([x[:, HD:] for x in blocks], axis=1)
        values.append(jnp.concatenate([top, bottom], axis=0))
    v_ref[...] = jnp.concatenate(values, axis=1).reshape(v_ref.shape)


def attend_forward(valid, in_ref, e_ref, ctx_ref, kaug, vaug, vt, kt, scores):
    sources = in_ref.shape[0]
    rows = in_ref.shape[1] * 2 // 5
    length = sources * rows
    per_block = QB // rows
    blocks = length // QB

    qk = in_ref[:, :rows, :].reshape(length, LANES).astype(F32)
    lane = lane_ids(qk.shape)
    position = lax.broadcasted_iota(jnp.int32, qk.shape, 0)
    bias = jnp.where(position < valid, 0.0, NEG)
    keys = jnp.where(lane < HD, swap_halves(qk), jnp.where(lane == HD, bias, 0.0))
    kaug[...] = keys.astype(BF16)
    half = in_ref[:, rows : rows * 3 // 2, :].astype(F32)
    swapped = swap_halves(half.reshape(length // 2, LANES)).reshape(half.shape)
    values = jnp.concatenate([half, swapped], axis=1).reshape(length, LANES)
    values = jnp.where(lane < HD, values, jnp.where(lane < HD + 2, 1.0, 0.0))
    vaug[...] = values.astype(BF16)
    vt[...] = values.T.astype(BF16)
    kt[...] = jnp.where(lane < HD, keys, 0.0).T.astype(BF16)

    def query_block(block):
        q = in_ref[pl.ds(block * per_block, per_block), :rows, :].reshape(QB, LANES).astype(F32)
        lane = lane_ids(q.shape)
        return jnp.where(lane < HD, q * 0.125, jnp.where(lane == HD, 1.0, 0.0)).astype(BF16)

    def score(slot, q, c):
        part = slice(c * KC, (c + 1) * KC)
        s = lax.dot_general(kaug[part, :], q, (((1,), (1,)), ((), ())), preferred_element_type=F32)
        scores[slot, part, :] = s
        return jnp.max(s, axis=0, keepdims=True)

    def weigh(block, slot, top, c):
        part = slice(c * KC, (c + 1) * KC)
        e = jnp.exp2((scores[slot, part, :] - top) * LOG2E).astype(BF16)
        e_ref[block, part, :] = e
        return jnp.dot(vt[:, part], e, preferred_element_type=F32)

    def finish(block, total):
        inverse = 1.0 / total[HD : HD + 1, :]
        row = lax.broadcasted_iota(jnp.int32, total.shape, 0)
        total = jnp.where(row < HD, total, 1.0) * inverse
        ctx_ref[pl.ds(pl.multiple_of(block * QB, QB), QB), :] = total.T

    chunks = range(length // KC)
    q = query_block(0)
    top = None
    for c in chunks:
        high = score(0, q, c)
        top = high if top is None else jnp.maximum(top, high)

    def step(block, top):
        slot = block % 2
        q = query_block(block + 1)
        total, later = None, None
        for c in chunks:
            high = score(1 - slot, q, c)
            term = weigh(block, slot, top, c)
            total = term if total is None else total + term
            later = high if later is None else jnp.maximum(later, high)
        finish(block, total)
        return later

    top = lax.fori_loop(0, blocks - 1, step, top)
    total = None
    for c in chunks:
        term = weigh(blocks - 1, (blocks - 1) % 2, top, c)
        total = term if total is None else total + term
    finish(blocks - 1, total)


def convolve(valid, in_ref, ctx_ref, taps_ref, part_ref, field, grad, hid, cot, bo, sums_ref):
    sources = in_ref.shape[0]
    rows = in_ref.shape[1] * 2 // 5
    first = rows * 3 // 2
    length = sources * rows
    half = length // 2
    mid = sources // 2
    step = CONV_ROWS
    steps = half // step
    lane = lane_ids((half, LANES))
    fc_low = in_ref[:mid, first:, :].reshape(half, LANES).astype(F32)
    fc_high = in_ref[mid:, first:, :].reshape(half, LANES).astype(F32)
    features = jnp.where(lane < HD, fc_low, swap_halves(fc_high))
    cot[...] = jnp.where(lane < HD, swap_halves(fc_low), fc_high)
    ctx = jnp.where(lane < HD, ctx_ref[:half, :], swap_halves(ctx_ref[half:, :]))
    hidden = features + ctx.astype(BF16).astype(F32)
    hid[...] = hidden
    position = lax.broadcasted_iota(jnp.int32, (half, LANES), 0) + jnp.where(lane < HD, 0, half)
    masked = jnp.where(position < valid, hidden, 0.0).astype(BF16).astype(F32)
    small = lane_ids((PAD, LANES))
    field[PAD : PAD + half, :] = masked
    field[:PAD, :] = jnp.where(small < HD, 0.0, swap_halves(masked[half - PAD :, :]))
    field[PAD + half :, :] = jnp.where(small < HD, swap_halves(masked[:PAD, :]), 0.0)
    sums_ref[...] = jnp.zeros_like(sums_ref)
    bias = taps_ref[TAPS : TAPS + 1, :]

    def forward_step(i, carry):
        base = pl.multiple_of(i * step, step)
        out = jnp.broadcast_to(bias, (step, LANES))
        for k in range(TAPS):
            out = out + taps_ref[k : k + 1, :] * field[pl.ds(base + (k + 1), step), :]
        gate = 1.0 / (1.0 + jnp.exp(-out))
        bo[pl.ds(base, step), :] = hid[pl.ds(base, step), :] + out * gate
        g = cot[pl.ds(base, step), :] * gate * (1.0 + out * (1.0 - gate))
        grad[pl.ds(base + PAD, step), :] = g.astype(BF16).astype(F32)
        for k in range(TAPS):
            term = g * field[pl.ds(base + (k + 1), step), :]
            part = slice(8 * k, 8 * k + 8)
            sums_ref[part, :] += jnp.sum(term.reshape(step // 8, 8, LANES), axis=0)
        part = slice(8 * TAPS, 8 * TAPS + 8)
        sums_ref[part, :] += jnp.sum(g.reshape(step // 8, 8, LANES), axis=0)
        return carry

    lax.fori_loop(0, steps, forward_step, 0)
    folded = jnp.sum(sums_ref[...].reshape(TAPS + 1, 8, LANES), axis=1)
    folded = folded + swap_halves(folded)
    taps_half = (TAPS + 1) // 2
    part_lane = lane_ids((taps_half, LANES))
    part_ref[...] = jnp.where(part_lane < HD, folded[:taps_half], folded[taps_half:])
    grad[:PAD, :] = jnp.where(small < HD, 0.0, swap_halves(grad[half : half + PAD, :]))
    grad[PAD + half :, :] = jnp.where(small < HD, swap_halves(grad[PAD : 2 * PAD, :]), 0.0)


def conv_backward_kernel(frames_ref, grad, cot, bo, ctx_ref, taps_ref, out_ref, gaug_ref):
    valid = frames_ref[0]
    sources, rows, _ = out_ref.shape
    half = cot.shape[0]
    mid = sources // 2
    step = CONV_ROWS
    steps = half // step
    lane_step = lane_ids((step, LANES))
    rows_step = lax.broadcasted_iota(jnp.int32, (step, LANES), 0)
    place = rows_step + jnp.where(lane_step < HD, 0, half)
    per_step = step // rows

    def augmented(gf, context):
        inverse = context[:, HD : HD + 1]
        gn = (gf * (inverse * 0.125)).astype(BF16).astype(F32)
        delta = jnp.sum(jnp.where(lane_step < HD, gn * context, 0.0), axis=1, keepdims=True)
        upper = delta.astype(BF16).astype(F32)
        tail = jnp.where(lane_step == HD, -upper, jnp.where(lane_step == HD + 1, upper - delta, 0.0))
        return jnp.where(lane_step < HD, gn, tail).astype(BF16)

    def backward_step(i, carry):
        base = pl.multiple_of(i * step, step)
        out = None
        for k in range(TAPS):
            term = taps_ref[k : k + 1, :] * grad[pl.ds(base + (TAPS - k), step), :]
            out = term if out is None else out + term
        out = jnp.where(place + base < valid, out, 0.0)
        gf = (cot[pl.ds(base, step), :] + out).astype(BF16).astype(F32)
        swapped = swap_halves(gf)
        block = bo[pl.ds(base, step), :]
        low = jnp.where(lane_step < HD, block, swapped).astype(BF16)
        high = jnp.where(lane_step < HD, swap_halves(block), gf).astype(BF16)
        at = i * per_step
        out_ref[pl.ds(at, per_step), :, :] = low.reshape(per_step, rows, LANES)
        out_ref[pl.ds(mid + at, per_step), :, :] = high.reshape(per_step, rows, LANES)
        gaug_ref[pl.ds(base, step), :] = augmented(gf, ctx_ref[pl.ds(base, step), :])
        other = pl.multiple_of(base + half, step)
        gaug_ref[pl.ds(other, step), :] = augmented(swapped, ctx_ref[pl.ds(other, step), :])
        return carry

    lax.fori_loop(0, steps, backward_step, 0)


def backward_kernel(in_ref, e_ref, gaug_ref, vaug, kt, bogf_ref, out_ref, acc):
    sources = in_ref.shape[0]
    rows = in_ref.shape[1] * 2 // 5
    length = sources * rows
    per_block = QB // rows
    chunks = length // KC
    acc[...] = jnp.zeros_like(acc)
    out_ref[:, rows * 3 // 2 :, :] = bogf_ref[...]

    def step(block, carry):
        q = in_ref[pl.ds(block * per_block, per_block), :rows, :].reshape(QB, LANES).astype(F32)
        g = gaug_ref[pl.ds(pl.multiple_of(block * QB, QB), QB), :]
        lane = lane_ids(q.shape)
        right = jnp.where(lane < HD, 0.0, swap_halves(q)).astype(BF16)
        left = jnp.where(lane < HD, g.astype(F32), 0.0).astype(BF16)

        def spread(c):
            return lax.dot_general(
                vaug[c * KC : (c + 1) * KC, :],
                g,
                (((1,), (1,)), ((), ())),
                preferred_element_type=F32,
            )

        total = None
        dp = spread(0)
        for c in range(chunks):
            part = slice(c * KC, (c + 1) * KC)
            e = e_ref[block, part, :]
            ds = (e.astype(F32) * dp).astype(BF16)
            if c + 1 < chunks:
                dp = spread(c + 1)
            acc[part, :] += jnp.dot(e, left, preferred_element_type=F32) + jnp.dot(
                ds, right, preferred_element_type=F32
            )
            term = jnp.dot(kt[:, part], ds, preferred_element_type=F32)
            total = term if total is None else total + term
        at = pl.ds(block * per_block, per_block)
        out_ref[at, :rows, :] = total.T.astype(BF16).reshape(per_block, rows, LANES)
        return carry

    lax.fori_loop(0, length // QB, step, 0)
    both = acc[...].reshape(sources, rows, LANES)
    lane = lane_ids(both.shape)
    gq = out_ref[:, :rows, :].astype(F32)
    out_ref[:, :rows, :] = jnp.where(lane < HD, gq, both).astype(BF16)
    half = rows // 2
    upper = swap_halves(both[:, half:, :].reshape(length // 2, LANES)).reshape(sources, half, LANES)
    gv = jnp.where(lane_ids(upper.shape) < HD, both[:, :half, :], upper) * 8.0
    out_ref[:, rows : rows * 3 // 2, :] = gv.astype(BF16)


def forward_kernel(
    frames_ref,
    in_ref,
    taps_ref,
    e_ref,
    vaug,
    kt,
    ctx_ref,
    grad,
    cot,
    bo,
    part_ref,
    scores,
    kaug,
    vt,
    field,
    hid,
    sums_ref,
):
    valid = frames_ref[0]
    attend_forward(valid, in_ref, e_ref, ctx_ref, kaug, vaug, vt, kt, scores)
    convolve(valid, in_ref, ctx_ref, taps_ref, part_ref, field, grad, hid, cot, bo, sums_ref)


def params_kernel(place_ref, same_ref, other_ref, taps_ref, bias_ref, heads):
    place = place_ref[0]
    core, x, half = place % 2, place // 2 % 4, place // 8 % 2
    for n, part in enumerate((same_ref, other_ref)):
        for i in range(part.shape[0]):
            for j in range(part.shape[1]):
                head = (half + n) % 2 * 8 + (x + 4 - i) % 4 * 2 + (core + j) % 2
                heads[head] = part[i, j]
    rows = heads.shape[1]
    for h in range(0, HEADS, 2):
        lanes = slice(h * HD, (h + 2) * HD)
        a = heads[h]
        b = heads[h + 1]
        low = lane_pair(a[:, :HD], b[:, :HD])
        high = lane_pair(a[:, HD:], b[:, HD:])
        taps_ref[:rows, lanes] = low
        taps_ref[rows:, lanes] = high[: TAPS - rows]
        bias_ref[:, lanes] = high[TAPS - rows :]


def shape_of(*dims, dtype=BF16):
    return jax.ShapeDtypeStruct(dims, dtype)


def pack(*fields):
    rows, utts, width = fields[0].shape
    return pl.pallas_call(
        pack_kernel,
        out_shape=shape_of(utts * HEADS, rows * 5 // 2, LANES),
        in_specs=[pl.BlockSpec(memory_space=pltpu.HBM)] * 5,
        out_specs=VMEM,
        scratch_shapes=[pltpu.VMEM((rows, utts, width), BF16)] * 5 + [pltpu.SemaphoreType.DMA((5,))],
        compiler_params=params(60),
        name="pack",
    )(*fields)


def unpack(field, rows, utts):
    return pl.pallas_call(
        unpack_kernel,
        out_shape=[shape_of(rows, utts, HEADS * HD)] * 5,
        in_specs=[VMEM],
        out_specs=[VMEM] * 5,
        compiler_params=params(24),
        name="unpack",
    )(field)


def forward(frames, field, taps):
    sources, tall, _ = field.shape
    rows = tall * 2 // 5
    length = sources * rows
    half = length // 2
    wide = (length, LANES)
    return pl.pallas_call(
        forward_kernel,
        out_shape=[
            shape_of(length // QB, length, QB),
            shape_of(*wide),
            shape_of(LANES, length),
            shape_of(*wide, dtype=F32),
            shape_of(half + 2 * PAD, LANES, dtype=F32),
            shape_of(half, LANES, dtype=F32),
            shape_of(half, LANES, dtype=F32),
            shape_of((TAPS + 1) // 2, LANES, dtype=F32),
        ],
        in_specs=[SMEM, VMEM, VMEM],
        out_specs=[VMEM] * 8,
        scratch_shapes=[
            pltpu.VMEM((2, length, QB), F32),
            pltpu.VMEM(wide, BF16),
            pltpu.VMEM((LANES, length), BF16),
            pltpu.VMEM((half + 2 * PAD, LANES), F32),
            pltpu.VMEM((half, LANES), F32),
            pltpu.VMEM((8 * (TAPS + 1), LANES), F32),
        ],
        compiler_params=params(36),
        cost_estimate=pl.CostEstimate(
            flops=8_000_000_000, bytes_accessed=20_000_000, transcendentals=4_000_000
        ),
        name="forward",
    )(frames, field, taps)


def conv_backward(frames, grad, cot, bo, ctx, taps, sources):
    length = ctx.shape[0]
    return pl.pallas_call(
        conv_backward_kernel,
        out_shape=[shape_of(sources, length // sources, LANES), shape_of(length, LANES)],
        in_specs=[SMEM] + [VMEM] * 5,
        out_specs=[VMEM] * 2,
        compiler_params=params(24),
        cost_estimate=pl.CostEstimate(
            flops=2_000_000_000, bytes_accessed=4_000_000, transcendentals=0
        ),
        name="conv_backward",
    )(frames, grad, cot, bo, ctx, taps)


def backward(field, e, gaug, vaug, kt, bogf):
    length = e.shape[1]
    return pl.pallas_call(
        backward_kernel,
        out_shape=shape_of(*field.shape),
        in_specs=[VMEM] * 6,
        out_specs=VMEM,
        scratch_shapes=[pltpu.VMEM((length, LANES), F32)],
        compiler_params=params(36),
        cost_estimate=pl.CostEstimate(
            flops=9_000_000_000, bytes_accessed=20_000_000, transcendentals=0
        ),
        name="backward",
    )(field, e, gaug, vaug, kt, bogf)


def unpack_params(place, parts):
    width = HEADS * HD
    taps, bias = pl.pallas_call(
        params_kernel,
        out_shape=[shape_of(TAPS, width, dtype=F32), shape_of(1, width, dtype=F32)],
        in_specs=[SMEM] + [VMEM] * len(parts),
        out_specs=[VMEM] * 2,
        scratch_shapes=[pltpu.VMEM((HEADS, *parts[0].shape[2:]), F32)],
        compiler_params=params(8),
        name="unpack_params",
    )(place.reshape(1), *parts)
    return taps, bias.reshape(width)


def exchange(field):
    return lax.all_to_all(field, "seq", split_axis=0, concat_axis=0, tiled=True)


def swap(field, axis, bit):
    count = lax.axis_size(axis)
    return lax.ppermute(field, axis, [(i, i ^ bit) for i in range(count)])


def along_x(field, steps):
    seq = lax.axis_size("seq")
    return lax.ppermute(field, "seq", [(i, i // 8 * 8 + (i + 2 * steps) % 8) for i in range(seq)])


def reduce_rest(part, place):
    for bit in (4, 8):
        part = part + swap(part, "dp", bit)
    part = jnp.stack([part, swap(part, "seq", 1)])
    part = jnp.stack([part] + [along_x(part, steps) for steps in (1, 2, 3)]).astype(BF16)
    wide = part.astype(F32)
    same = wide + swap(part, "seq", 16).astype(F32)
    other = swap(part, "seq", 8).astype(F32) + swap(part, "seq", 24).astype(F32)
    return unpack_params(place, [same, other])


def on_device(
    queries, key_vectors, value_vectors, features, cotangent, frames, conv_kernel, conv_bias
):
    rows, utts, _ = queries.shape
    item = lax.axis_index("seq")
    utt = item // HEADS
    head = item % HEADS
    valid = jnp.sum(jnp.where(jnp.arange(utts) == utt, frames, 0), keepdims=True)
    taps = jnp.concatenate([conv_kernel, conv_bias[None]], axis=0)
    taps = lax.dynamic_slice_in_dim(taps, head * HD, HD, axis=1)
    taps = jnp.concatenate([taps, taps], axis=1)

    field = exchange(pack(queries, key_vectors, value_vectors, features, cotangent))
    e, vaug, kt, ctx, grad, cot, bo, part = forward(valid, field, taps)
    near = swap(part, "dp", 1)
    bogf, gaug = conv_backward(valid, grad, cot, bo, ctx, taps, field.shape[0])
    gaug, part, near = lax.optimization_barrier((gaug, part, near))
    part = part + near
    near = swap(part, "dp", 2)
    field = backward(field, e, gaug, vaug, kt, bogf)
    field, part, near = lax.optimization_barrier((field, part, near))
    part = part + near
    field = exchange(field)
    grad_kernel, grad_bias = reduce_rest(part, item)
    grad_q, grad_k, grad_v, block_out, grad_features = unpack(field, rows, utts)
    return block_out, grad_features, grad_q, grad_k, grad_v, grad_kernel, grad_bias


def solution(mesh):
    field = P("seq", "dp", None)
    return jax.shard_map(
        on_device,
        mesh=mesh,
        in_specs=(field,) * 5 + (P("dp"), P(), P()),
        out_specs=(field,) * 5 + (P(), P()),
        check_vma=False,
    )
```

```python
import math

import jax
import jax.numpy as jnp
from jax import lax
from jax.experimental import pallas as pl
from jax.experimental.pallas import tpu as pltpu
from jax.sharding import PartitionSpec as P

HEADS = 16
TAPS = 31
HD = 64
LANES = 128
PAD = 16
QB = 1024
KC = 256
CONV_ROWS = 256
F32 = jnp.float32
BF16 = jnp.bfloat16
NEG = -1e30
LOG2E = math.log2(math.e)

VMEM = pl.BlockSpec(memory_space=pltpu.VMEM)
SMEM = pl.BlockSpec(memory_space=pltpu.SMEM)


def params(mib):
    return pltpu.CompilerParams(vmem_limit_bytes=mib * 1024 * 1024)


def lane_pair(low, high):
    return jnp.concatenate([low, high], axis=-1)


def swap_halves(x):
    return pltpu.roll(x, HD, x.ndim - 1)


def lane_ids(shape):
    return lax.broadcasted_iota(jnp.int32, shape, len(shape) - 1)


def pack_kernel(q_hbm, k_hbm, v_hbm, f_hbm, c_hbm, out_ref, q_ref, k_ref, v_ref, f_ref, c_ref, sems):
    pairs = ((q_hbm, q_ref), (k_hbm, k_ref), (v_hbm, v_ref), (f_hbm, f_ref), (c_hbm, c_ref))
    copies = [pltpu.make_async_copy(a, b, sems.at[n]) for n, (a, b) in enumerate(pairs)]
    for copy in copies:
        copy.start()
    rows, utts, width = q_ref.shape

    def one_head(field, u, h):
        return field[:, (u * HEADS + h) * HD : (u * HEADS + h + 1) * HD]

    def pair(a_ref, b_ref, first):
        a = a_ref[...].reshape(rows, utts * width)
        b = b_ref[...].reshape(rows, utts * width)
        for u in range(utts):
            for h in range(HEADS):
                out_ref[u * HEADS + h, first : first + rows, :] = lane_pair(
                    one_head(a, u, h), one_head(b, u, h)
                )

    copies[0].wait()
    copies[1].wait()
    pair(q_ref, k_ref, 0)
    copies[2].wait()
    values = v_ref[...].reshape(rows, utts * width)
    for u in range(utts):
        for h in range(HEADS):
            v = one_head(values, u, h)
            out_ref[u * HEADS + h, rows : rows * 3 // 2, :] = lane_pair(
                v[: rows // 2], v[rows // 2 :]
            )
    copies[3].wait()
    copies[4].wait()
    pair(f_ref, c_ref, rows * 3 // 2)


def unpack_kernel(in_ref, q_ref, k_ref, v_ref, f_ref, c_ref):
    rows, utts, _ = q_ref.shape

    def pair(a_ref, b_ref, first):
        firsts, seconds = [], []
        for u in range(utts):
            blocks = [in_ref[u * HEADS + h, first : first + rows, :] for h in range(HEADS)]
            firsts.append(jnp.concatenate([x[:, :HD] for x in blocks], axis=1))
            seconds.append(jnp.concatenate([x[:, HD:] for x in blocks], axis=1))
        a_ref[...] = jnp.concatenate(firsts, axis=1).reshape(a_ref.shape)
        b_ref[...] = jnp.concatenate(seconds, axis=1).reshape(b_ref.shape)

    pair(f_ref, c_ref, rows * 3 // 2)
    pair(q_ref, k_ref, 0)
    values = []
    for u in range(utts):
        blocks = [in_ref[u * HEADS + h, rows : rows * 3 // 2, :] for h in range(HEADS)]
        top = jnp.concatenate([x[:, :HD] for x in blocks], axis=1)
        bottom = jnp.concatenate([x[:, HD:] for x in blocks], axis=1)
        values.append(jnp.concatenate([top, bottom], axis=0))
    v_ref[...] = jnp.concatenate(values, axis=1).reshape(v_ref.shape)


def attend_forward(valid, in_ref, e_ref, ctx_ref, kaug, vaug, vt, kt, scores):
    sources = in_ref.shape[0]
    rows = in_ref.shape[1] * 2 // 5
    length = sources * rows
    per_block = QB // rows
    blocks = length // QB

    qk = in_ref[:, :rows, :].reshape(length, LANES).astype(F32)
    lane = lane_ids(qk.shape)
    position = lax.broadcasted_iota(jnp.int32, qk.shape, 0)
    bias = jnp.where(position < valid, 0.0, NEG)
    keys = jnp.where(lane < HD, swap_halves(qk), jnp.where(lane == HD, bias, 0.0))
    kaug[...] = keys.astype(BF16)
    half = in_ref[:, rows : rows * 3 // 2, :].astype(F32)
    swapped = swap_halves(half.reshape(length // 2, LANES)).reshape(half.shape)
    values = jnp.concatenate([half, swapped], axis=1).reshape(length, LANES)
    values = jnp.where(lane < HD, values, jnp.where(lane < HD + 2, 1.0, 0.0))
    vaug[...] = values.astype(BF16)
    vt[...] = values.T.astype(BF16)
    kt[...] = jnp.where(lane < HD, keys, 0.0).T.astype(BF16)

    def query_block(block):
        q = in_ref[pl.ds(block * per_block, per_block), :rows, :].reshape(QB, LANES).astype(F32)
        lane = lane_ids(q.shape)
        return jnp.where(lane < HD, q * 0.125, jnp.where(lane == HD, 1.0, 0.0)).astype(BF16)

    def score(slot, q, c):
        part = slice(c * KC, (c + 1) * KC)
        s = lax.dot_general(kaug[part, :], q, (((1,), (1,)), ((), ())), preferred_element_type=F32)
        scores[slot, part, :] = s
        return jnp.max(s, axis=0, keepdims=True)

    def weigh(block, slot, top, c):
        part = slice(c * KC, (c + 1) * KC)
        e = jnp.exp2((scores[slot, part, :] - top) * LOG2E).astype(BF16)
        e_ref[block, part, :] = e
        return jnp.dot(vt[:, part], e, preferred_element_type=F32)

    def finish(block, total):
        inverse = 1.0 / total[HD : HD + 1, :]
        row = lax.broadcasted_iota(jnp.int32, total.shape, 0)
        total = jnp.where(row < HD, total, 1.0) * inverse
        ctx_ref[pl.ds(pl.multiple_of(block * QB, QB), QB), :] = total.T

    chunks = range(length // KC)
    q = query_block(0)
    top = None
    for c in chunks:
        high = score(0, q, c)
        top = high if top is None else jnp.maximum(top, high)

    def step(block, top):
        slot = block % 2
        q = query_block(block + 1)
        total, later = None, None
        for c in chunks:
            high = score(1 - slot, q, c)
            term = weigh(block, slot, top, c)
            total = term if total is None else total + term
            later = high if later is None else jnp.maximum(later, high)
        finish(block, total)
        return later

    top = lax.fori_loop(0, blocks - 1, step, top)
    total = None
    for c in chunks:
        term = weigh(blocks - 1, (blocks - 1) % 2, top, c)
        total = term if total is None else total + term
    finish(blocks - 1, total)


def convolve(valid, in_ref, ctx_ref, taps_ref, part_ref, field, grad, hid, cot, bo, sums_ref):
    sources = in_ref.shape[0]
    rows = in_ref.shape[1] * 2 // 5
    first = rows * 3 // 2
    length = sources * rows
    half = length // 2
    mid = sources // 2
    step = CONV_ROWS
    steps = half // step
    lane = lane_ids((half, LANES))
    fc_low = in_ref[:mid, first:, :].reshape(half, LANES).astype(F32)
    fc_high = in_ref[mid:, first:, :].reshape(half, LANES).astype(F32)
    features = jnp.where(lane < HD, fc_low, swap_halves(fc_high))
    cot[...] = jnp.where(lane < HD, swap_halves(fc_low), fc_high)
    ctx = jnp.where(lane < HD, ctx_ref[:half, :], swap_halves(ctx_ref[half:, :]))
    hidden = features + ctx.astype(BF16).astype(F32)
    hid[...] = hidden
    position = lax.broadcasted_iota(jnp.int32, (half, LANES), 0) + jnp.where(lane < HD, 0, half)
    masked = jnp.where(position < valid, hidden, 0.0).astype(BF16).astype(F32)
    small = lane_ids((PAD, LANES))
    field[PAD : PAD + half, :] = masked
    field[:PAD, :] = jnp.where(small < HD, 0.0, swap_halves(masked[half - PAD :, :]))
    field[PAD + half :, :] = jnp.where(small < HD, swap_halves(masked[:PAD, :]), 0.0)
    sums_ref[...] = jnp.zeros_like(sums_ref)
    bias = taps_ref[TAPS : TAPS + 1, :]

    def forward_step(i, carry):
        base = pl.multiple_of(i * step, step)
        out = jnp.broadcast_to(bias, (step, LANES))
        for k in range(TAPS):
            out = out + taps_ref[k : k + 1, :] * field[pl.ds(base + (k + 1), step), :]
        gate = 1.0 / (1.0 + jnp.exp(-out))
        bo[pl.ds(base, step), :] = hid[pl.ds(base, step), :] + out * gate
        g = cot[pl.ds(base, step), :] * gate * (1.0 + out * (1.0 - gate))
        grad[pl.ds(base + PAD, step), :] = g.astype(BF16).astype(F32)
        for k in range(TAPS):
            term = g * field[pl.ds(base + (k + 1), step), :]
            part = slice(8 * k, 8 * k + 8)
            sums_ref[part, :] += jnp.sum(term.reshape(step // 8, 8, LANES), axis=0)
        part = slice(8 * TAPS, 8 * TAPS + 8)
        sums_ref[part, :] += jnp.sum(g.reshape(step // 8, 8, LANES), axis=0)
        return carry

    lax.fori_loop(0, steps, forward_step, 0)
    folded = jnp.sum(sums_ref[...].reshape(TAPS + 1, 8, LANES), axis=1)
    folded = folded + swap_halves(folded)
    taps_half = (TAPS + 1) // 2
    part_lane = lane_ids((taps_half, LANES))
    part_ref[...] = jnp.where(part_lane < HD, folded[:taps_half], folded[taps_half:])
    grad[:PAD, :] = jnp.where(small < HD, 0.0, swap_halves(grad[half : half + PAD, :]))
    grad[PAD + half :, :] = jnp.where(small < HD, swap_halves(grad[PAD : 2 * PAD, :]), 0.0)


def conv_backward_kernel(frames_ref, grad, cot, bo, ctx_ref, taps_ref, out_ref, gaug_ref):
    valid = frames_ref[0]
    sources, rows, _ = out_ref.shape
    half = cot.shape[0]
    mid = sources // 2
    step = CONV_ROWS
    steps = half // step
    lane_step = lane_ids((step, LANES))
    rows_step = lax.broadcasted_iota(jnp.int32, (step, LANES), 0)
    place = rows_step + jnp.where(lane_step < HD, 0, half)
    per_step = step // rows

    def augmented(gf, context):
        inverse = context[:, HD : HD + 1]
        gn = (gf * (inverse * 0.125)).astype(BF16).astype(F32)
        delta = jnp.sum(jnp.where(lane_step < HD, gn * context, 0.0), axis=1, keepdims=True)
        upper = delta.astype(BF16).astype(F32)
        tail = jnp.where(lane_step == HD, -upper, jnp.where(lane_step == HD + 1, upper - delta, 0.0))
        return jnp.where(lane_step < HD, gn, tail).astype(BF16)

    def backward_step(i, carry):
        base = pl.multiple_of(i * step, step)
        out = None
        for k in range(TAPS):
            term = taps_ref[k : k + 1, :] * grad[pl.ds(base + (TAPS - k), step), :]
            out = term if out is None else out + term
        out = jnp.where(place + base < valid, out, 0.0)
        gf = (cot[pl.ds(base, step), :] + out).astype(BF16).astype(F32)
        swapped = swap_halves(gf)
        block = bo[pl.ds(base, step), :]
        low = jnp.where(lane_step < HD, block, swapped).astype(BF16)
        high = jnp.where(lane_step < HD, swap_halves(block), gf).astype(BF16)
        at = i * per_step
        out_ref[pl.ds(at, per_step), :, :] = low.reshape(per_step, rows, LANES)
        out_ref[pl.ds(mid + at, per_step), :, :] = high.reshape(per_step, rows, LANES)
        gaug_ref[pl.ds(base, step), :] = augmented(gf, ctx_ref[pl.ds(base, step), :])
        other = pl.multiple_of(base + half, step)
        gaug_ref[pl.ds(other, step), :] = augmented(swapped, ctx_ref[pl.ds(other, step), :])
        return carry

    lax.fori_loop(0, steps, backward_step, 0)


def backward_kernel(in_ref, e_ref, gaug_ref, vaug, kt, bogf_ref, out_ref, acc):
    sources = in_ref.shape[0]
    rows = in_ref.shape[1] * 2 // 5
    length = sources * rows
    per_block = QB // rows
    chunks = length // KC
    acc[...] = jnp.zeros_like(acc)
    out_ref[:, rows * 3 // 2 :, :] = bogf_ref[...]

    def step(block, carry):
        q = in_ref[pl.ds(block * per_block, per_block), :rows, :].reshape(QB, LANES).astype(F32)
        g = gaug_ref[pl.ds(pl.multiple_of(block * QB, QB), QB), :]
        lane = lane_ids(q.shape)
        right = jnp.where(lane < HD, 0.0, swap_halves(q)).astype(BF16)
        left = jnp.where(lane < HD, g.astype(F32), 0.0).astype(BF16)

        def spread(c):
            return lax.dot_general(
                vaug[c * KC : (c + 1) * KC, :],
                g,
                (((1,), (1,)), ((), ())),
                preferred_element_type=F32,
            )

        total = None
        dp = spread(0)
        for c in range(chunks):
            part = slice(c * KC, (c + 1) * KC)
            e = e_ref[block, part, :]
            ds = (e.astype(F32) * dp).astype(BF16)
            if c + 1 < chunks:
                dp = spread(c + 1)
            acc[part, :] += jnp.dot(e, left, preferred_element_type=F32) + jnp.dot(
                ds, right, preferred_element_type=F32
            )
            term = jnp.dot(kt[:, part], ds, preferred_element_type=F32)
            total = term if total is None else total + term
        at = pl.ds(block * per_block, per_block)
        out_ref[at, :rows, :] = total.T.astype(BF16).reshape(per_block, rows, LANES)
        return carry

    lax.fori_loop(0, length // QB, step, 0)
    both = acc[...].reshape(sources, rows, LANES)
    lane = lane_ids(both.shape)
    gq = out_ref[:, :rows, :].astype(F32)
    out_ref[:, :rows, :] = jnp.where(lane < HD, gq, both).astype(BF16)
    half = rows // 2
    upper = swap_halves(both[:, half:, :].reshape(length // 2, LANES)).reshape(sources, half, LANES)
    gv = jnp.where(lane_ids(upper.shape) < HD, both[:, :half, :], upper) * 8.0
    out_ref[:, rows : rows * 3 // 2, :] = gv.astype(BF16)


def forward_kernel(
    frames_ref,
    in_ref,
    taps_ref,
    e_ref,
    vaug,
    kt,
    ctx_ref,
    grad,
    cot,
    bo,
    part_ref,
    scores,
    kaug,
    vt,
    field,
    hid,
    sums_ref,
):
    valid = frames_ref[0]
    attend_forward(valid, in_ref, e_ref, ctx_ref, kaug, vaug, vt, kt, scores)
    convolve(valid, in_ref, ctx_ref, taps_ref, part_ref, field, grad, hid, cot, bo, sums_ref)


def params_kernel(place_ref, parts_ref, taps_ref, bias_ref, heads):
    place = place_ref[0]
    core, x, half = place % 2, place // 2 % 4, place // 8 % 2
    for i in range(parts_ref.shape[0]):
        for j in range(parts_ref.shape[1]):
            for n in range(parts_ref.shape[2]):
                head = (half + n) % 2 * 8 + (x + 4 - i) % 4 * 2 + (core + j) % 2
                heads[head] = parts_ref[i, j, n]
    rows = heads.shape[1]
    for h in range(0, HEADS, 2):
        lanes = slice(h * HD, (h + 2) * HD)
        a = heads[h]
        b = heads[h + 1]
        low = lane_pair(a[:, :HD], b[:, :HD])
        high = lane_pair(a[:, HD:], b[:, HD:])
        taps_ref[:rows, lanes] = low
        taps_ref[rows:, lanes] = high[: TAPS - rows]
        bias_ref[:, lanes] = high[TAPS - rows :]


def shape_of(*dims, dtype=BF16):
    return jax.ShapeDtypeStruct(dims, dtype)


def pack(*fields):
    rows, utts, width = fields[0].shape
    return pl.pallas_call(
        pack_kernel,
        out_shape=shape_of(utts * HEADS, rows * 5 // 2, LANES),
        in_specs=[pl.BlockSpec(memory_space=pltpu.HBM)] * 5,
        out_specs=VMEM,
        scratch_shapes=[pltpu.VMEM((rows, utts, width), BF16)] * 5 + [pltpu.SemaphoreType.DMA((5,))],
        compiler_params=params(60),
        name="pack",
    )(*fields)


def unpack(field, rows, utts):
    return pl.pallas_call(
        unpack_kernel,
        out_shape=[shape_of(rows, utts, HEADS * HD)] * 5,
        in_specs=[VMEM],
        out_specs=[VMEM] * 5,
        compiler_params=params(24),
        name="unpack",
    )(field)


def forward(frames, field, taps):
    sources, tall, _ = field.shape
    rows = tall * 2 // 5
    length = sources * rows
    half = length // 2
    wide = (length, LANES)
    return pl.pallas_call(
        forward_kernel,
        out_shape=[
            shape_of(length // QB, length, QB),
            shape_of(*wide),
            shape_of(LANES, length),
            shape_of(*wide, dtype=F32),
            shape_of(half + 2 * PAD, LANES, dtype=F32),
            shape_of(half, LANES, dtype=F32),
            shape_of(half, LANES, dtype=F32),
            shape_of((TAPS + 1) // 2, LANES, dtype=F32),
        ],
        in_specs=[SMEM, VMEM, VMEM],
        out_specs=[VMEM] * 8,
        scratch_shapes=[
            pltpu.VMEM((2, length, QB), F32),
            pltpu.VMEM(wide, BF16),
            pltpu.VMEM((LANES, length), BF16),
            pltpu.VMEM((half + 2 * PAD, LANES), F32),
            pltpu.VMEM((half, LANES), F32),
            pltpu.VMEM((8 * (TAPS + 1), LANES), F32),
        ],
        compiler_params=params(36),
        cost_estimate=pl.CostEstimate(
            flops=8_000_000_000, bytes_accessed=20_000_000, transcendentals=4_000_000
        ),
        name="forward",
    )(frames, field, taps)


def conv_backward(frames, grad, cot, bo, ctx, taps, sources):
    length = ctx.shape[0]
    return pl.pallas_call(
        conv_backward_kernel,
        out_shape=[shape_of(sources, length // sources, LANES), shape_of(length, LANES)],
        in_specs=[SMEM] + [VMEM] * 5,
        out_specs=[VMEM] * 2,
        compiler_params=params(24),
        cost_estimate=pl.CostEstimate(
            flops=2_000_000_000, bytes_accessed=4_000_000, transcendentals=0
        ),
        name="conv_backward",
    )(frames, grad, cot, bo, ctx, taps)


def backward(field, e, gaug, vaug, kt, bogf):
    length = e.shape[1]
    return pl.pallas_call(
        backward_kernel,
        out_shape=shape_of(*field.shape),
        in_specs=[VMEM] * 6,
        out_specs=VMEM,
        scratch_shapes=[pltpu.VMEM((length, LANES), F32)],
        compiler_params=params(36),
        cost_estimate=pl.CostEstimate(
            flops=9_000_000_000, bytes_accessed=20_000_000, transcendentals=0
        ),
        name="backward",
    )(field, e, gaug, vaug, kt, bogf)


def unpack_params(place, parts):
    width = HEADS * HD
    taps, bias = pl.pallas_call(
        params_kernel,
        out_shape=[shape_of(TAPS, width, dtype=F32), shape_of(1, width, dtype=F32)],
        in_specs=[SMEM, VMEM],
        out_specs=[VMEM] * 2,
        scratch_shapes=[pltpu.VMEM((HEADS, *parts.shape[3:]), F32)],
        compiler_params=params(8),
        name="unpack_params",
    )(place.reshape(1), parts)
    return taps, bias.reshape(width)


def exchange(field):
    return lax.all_to_all(field, "seq", split_axis=0, concat_axis=0, tiled=True)


def swap(field, axis, bit):
    count = lax.axis_size(axis)
    return lax.ppermute(field, axis, [(i, i ^ bit) for i in range(count)])


def along_x(field, steps):
    seq = lax.axis_size("seq")
    return lax.ppermute(field, "seq", [(i, i // 8 * 8 + (i + 2 * steps) % 8) for i in range(seq)])


def reduce_rest(part, place):
    for bit in (4, 8):
        part = part + swap(part, "dp", bit)
    part = jnp.stack([part, swap(part, "seq", 1)])
    part = jnp.stack([part] + [along_x(part, steps) for steps in (1, 2, 3)]).astype(BF16)
    wide = part.astype(F32)
    first, second, third = [swap(part, "dp", bit).astype(F32) for bit in (1, 2, 3)]
    return unpack_params(place, (wide + first) + (second + third))


def on_device(
    queries, key_vectors, value_vectors, features, cotangent, frames, conv_kernel, conv_bias
):
    rows, utts, _ = queries.shape
    item = lax.axis_index("seq")
    utt = item // HEADS
    head = item % HEADS
    valid = jnp.sum(jnp.where(jnp.arange(utts) == utt, frames, 0), keepdims=True)
    taps = jnp.concatenate([conv_kernel, conv_bias[None]], axis=0)
    taps = lax.dynamic_slice_in_dim(taps, head * HD, HD, axis=1)
    taps = jnp.concatenate([taps, taps], axis=1)

    field = exchange(pack(queries, key_vectors, value_vectors, features, cotangent))
    e, vaug, kt, ctx, grad, cot, bo, part = forward(valid, field, taps)
    near = swap(part, "seq", 16)
    bogf, gaug = conv_backward(valid, grad, cot, bo, ctx, taps, field.shape[0])
    gaug, part, near = lax.optimization_barrier((gaug, part, near))
    part = part + near
    near = swap(part, "seq", 8)
    field = backward(field, e, gaug, vaug, kt, bogf)
    field, part, near = lax.optimization_barrier((field, part, near))
    part = jnp.stack([part, near])
    field = exchange(field)
    grad_kernel, grad_bias = reduce_rest(part, item)
    grad_q, grad_k, grad_v, block_out, grad_features = unpack(field, rows, utts)
    return block_out, grad_features, grad_q, grad_k, grad_v, grad_kernel, grad_bias


def solution(mesh):
    field = P("seq", "dp", None)
    return jax.shard_map(
        on_device,
        mesh=mesh,
        in_specs=(field,) * 5 + (P("dp"), P(), P()),
        out_specs=(field,) * 5 + (P(), P()),
        check_vma=False,
    )
```
